512 devices in a mesh: blk: 64 (over x, z_lo, core), head: 4 (over y), seq: 2 (over z_hi).
Axes of the slice: x: 4, y: 4, z: 16 (z_hi: 2, z_lo: 8; z = z_hi * 8 + z_lo), core: 2. Of those that a mesh axis runs over, the one named last changes fastest.
Arguments:
- query_rows: bfloat16 [16384, 2048], P(('seq', 'blk'), 'head'), parts along dimension 0, may hold values from -6 to 6
- key_rows: bfloat16 [16384, 2048], P(('seq', 'blk'), 'head'), parts along dimension 0, may hold values from -6 to 6
- value_rows: bfloat16 [16384, 2048], P(('seq', 'blk'), 'head'), parts along dimension 0, may hold values from -6 to 6
- kerple_power: float32 [16], P('head'), may hold values from 0.05 to 2
- kerple_scale: float32 [16], P('head'), may hold values from 0.1 to 4
- doc_lengths: int32 [8], P('seq'), parts along dimension 0, may hold values from 1 to 4096, 8192 in all
Outputs:
- attended: bfloat16 [16384, 2048], P(('seq', 'blk'), 'head'), parts along dimension 0
The draws below stay inside these ranges and needn't reach their ends.
There are 2 independent parts, one for each index of `seq`. The reference program is written for one: setup_inputs(seed, part) draws one part's arguments, and reference() takes and returns one part's arrays. A program takes and returns all parts, laid end to end along the dimension named above; an argument that names none is the same for every part. Nothing has to cross between parts.
Inputs may be any that keep to these rules, and one draw needn't show every extreme that they name: `doc_lengths`: the lengths sum to 8192; the largest equals 4096.
All inputs are finite; a program needn't handle non-finite values.
Results may differ from the reference program's by a relative error of at most 0.0045.
Values may be sent and summed in bfloat16 or wider, within the bound.
A program may use at most 64 MiB of HBM per device.

```python
import math
import jax
import jax.numpy as jnp
import numpy as np
from jax import lax

HEADS = 16
HEAD_DIM = 128
DOCS = 4
TOKENS = 8192


def draw_query_rows(key, part):
    key = jax.random.fold_in(key, 11)
    drawn = jnp.clip(jax.random.normal(key, (TOKENS, HEADS * HEAD_DIM), jnp.float32), -6.0, 6.0)
    return drawn.astype(jnp.bfloat16)


def draw_key_rows(key, part):
    key = jax.random.fold_in(key, 17)
    drawn = jnp.clip(jax.random.normal(key, (TOKENS, HEADS * HEAD_DIM), jnp.float32), -6.0, 6.0)
    return drawn.astype(jnp.bfloat16)


def draw_kerple_power(key, part):
    key = jax.random.fold_in(key, 23)
    first_key = jax.random.fold_in(key, 0)
    drawn = jnp.exp(jax.random.uniform(first_key, (HEADS,), jnp.float32, math.log(0.05), math.log(2.0)))
    return drawn.astype(jnp.float32)


def levels(stream_key, shape, cuts, least, largest):
    def one(axis_at, shards_of):
        draws = jax.random.uniform(jax.random.fold_in(jax.random.fold_in(stream_key, 6), axis_at), (shards_of,), jnp.float32, least / len(cuts), largest / len(cuts))
        return jnp.repeat(jnp.exp(draws), shape[axis_at] // shards_of).reshape((-1,) + (1,) * (len(shape) - axis_at - 1))

    loudness = one(*cuts[0])
    for cut in cuts[1:]:
        loudness = loudness * one(*cut)
    return loudness


def split_up(count, total, reach, lean):
    portions = [(1 << 20) // math.isqrt(rank ** lean) + 1 for rank in range(2, count + 1)]
    spare, counts = total - reach - (count - 1), [1] * (count - 1)
    while spare > 0:
        candidates = [i for i in range(count - 1) if counts[i] < reach]
        pool, left = sum([portions[i] for i in candidates]), spare
        for i in candidates:
            extra = min(reach - counts[i], max(1, left * portions[i] // pool), spare)
            counts[i] = counts[i] + extra
            spare = spare - extra
    return np.array([reach] + counts)


def ragged(key, number_of, total, reach, lean):
    if number_of == 2:
        one = jax.random.randint(key, (), max(1, total - reach), min(reach, total - 1) + 1)
        return jnp.stack([one, total - one])
    sizes = jnp.asarray(split_up(number_of, total, reach, lean), jnp.int32)
    twos = (number_of - 1) // 2
    giver, receiver = sizes[1:1 + 2 * twos:2], sizes[2:2 + 2 * twos:2]
    margin = jnp.minimum(giver - 1, reach - receiver)
    moved = jax.random.randint(jax.random.fold_in(key, 1), (twos,), 0, 1 << 20) % (margin + 1)
    sizes = sizes.at[1:1 + 2 * twos:2].set(giver - moved).at[2:2 + 2 * twos:2].set(receiver + moved)
    return sizes[jax.random.permutation(jax.random.fold_in(key, 2), number_of)]


def normal_values(key, dims, deviation, bound, cuts=(), held_as=jnp.bfloat16):
    values = jax.random.normal(key, dims, jnp.float32) * deviation
    if len(cuts) > 0:
        values = levels(key, dims, cuts, -0.22, 0.18) * values
    return jnp.clip(values, min=-bound, max=bound).astype(held_as)


def setup_inputs(seed: int = 0, part: int = 0) -> dict:
    splits = jax.random.split(jax.random.key(seed), 7)
    part_keys = jax.random.split(jax.random.fold_in(splits[6], part), 7)
    query_rows = draw_query_rows(jax.random.fold_in(jax.random.fold_in(splits[6], part), 71), part)
    key_rows = draw_key_rows(jax.random.fold_in(jax.random.fold_in(splits[6], part), 71), part)
    value_rows = normal_values(part_keys[2], (TOKENS, HEADS * HEAD_DIM), 1.0, 6.0, ((0, 64), (1, 4)))
    kerple_power = draw_kerple_power(jax.random.fold_in(splits[6], 71), part)
    kerple_scale = jnp.clip(jnp.exp(math.log(4.0) - 3.6888794 * jax.random.uniform(splits[4], (HEADS,), jnp.float32) ** levels(splits[4], (HEADS,), ((0, 4),), -0.2, 0.2)), 0.1, 4.0)
    doc_lengths = ragged(part_keys[5], DOCS, TOKENS, TOKENS // 2, 2).astype(jnp.int32)
    return {"query_rows": query_rows, "key_rows": key_rows, "value_rows": value_rows, "kerple_power": kerple_power, "kerple_scale": kerple_scale, "doc_lengths": doc_lengths}


NEG_FILL = -1e+30

def reference(query_rows, key_rows, value_rows, kerple_power, kerple_scale, doc_lengths):
    doc_ends = jnp.cumsum(doc_lengths)
    positions = jnp.arange(TOKENS, dtype=jnp.int32)
    doc_ids = lax.optimization_barrier(jnp.sum((positions[:, None] >= doc_ends[None, :]).astype(jnp.int32), axis=1))
    distance = positions[:, None] - positions[None, :]
    visible = (distance >= 0) & (doc_ids[:, None] == doc_ids[None, :])
    span = jnp.maximum(distance, 0).astype(jnp.float32)
    q_heads = query_rows.reshape(TOKENS, HEADS, HEAD_DIM).transpose(1, 0, 2)
    k_heads = key_rows.reshape(TOKENS, HEADS, HEAD_DIM).transpose(1, 0, 2)
    v_heads = value_rows.reshape(TOKENS, HEADS, HEAD_DIM).transpose(1, 0, 2)

    def one_head(pieces):
        q_head, k_head, v_head, power, scale = pieces
        scores = jnp.dot(q_head, k_head.T, preferred_element_type=jnp.float32) / math.sqrt(HEAD_DIM)
        kerple_bias = -power * jnp.log1p(scale * span)
        shifted = jnp.where(visible, scores + kerple_bias, NEG_FILL)
        row_top = lax.optimization_barrier(jnp.max(shifted, axis=1, keepdims=True))
        weights = jnp.where(visible, jnp.exp(shifted - row_top), 0.0)
        row_total = lax.optimization_barrier(jnp.sum(weights, axis=1, keepdims=True))
        summed = jnp.dot(weights.astype(jnp.bfloat16), v_head, preferred_element_type=jnp.float32)
        return summed / row_total
    outputs = lax.map(one_head, (q_heads, k_heads, v_heads, kerple_power, kerple_scale))
    return outputs.transpose(1, 0, 2).reshape(TOKENS, HEADS * HEAD_DIM).astype(jnp.bfloat16)
```

```python
import functools
import math

import jax
import jax.numpy as jnp
from jax import lax
from jax.experimental import pallas as pl
from jax.experimental.pallas import tpu as pltpu
from jax.sharding import PartitionSpec as P

MESH = pl.DeviceIdType.MESH
NEG = -1e30
TINY = 1e-30
SIDE = 4
CELL = SIDE * SIDE
LOG2E = math.log2(math.e)


def kernel(
    rows,
    width,
    count,
    power_ref,
    scale_ref,
    lengths_ref,
    q_ref,
    k_ref,
    v_ref,
    out_ref,
    qcat,
    kcat,
    vbuf,
    acc,
    top,
    tot,
    table,
    part_out,
    stat_out,
    part_in,
    stat_in,
    merged,
    deal_send,
    deal_recv,
    pass_send,
    pass_recv,
    share_send,
    share_recv,
    part_send,
    part_recv,
    stat_send,
    stat_recv,
    back_send,
    back_recv,
):
    me = lax.axis_index("blk")
    cell = me // CELL
    base = cell * CELL
    place = me - base
    head = place // SIDE
    mine = place % SIDE
    quarter = base + head * SIDE
    span = SIDE * rows

    barrier = pltpu.get_barrier_semaphore()

    def greet(step, _):
        other = base + lax.rem(place + step, CELL)
        pl.semaphore_signal(barrier, inc=1, device_id={"blk": other}, device_id_type=MESH)
        return 0

    lax.fori_loop(1, CELL, greet, 0)
    peers = CELL - 1
    for hop in (-2, -1, 1, 2):
        other = me + hop * CELL
        there = (other >= 0) & (other < count)
        peers = peers + there.astype(jnp.int32)

        @pl.when(there)
        def _():
            pl.semaphore_signal(barrier, inc=1, device_id={"blk": other}, device_id_type=MESH)

    pl.semaphore_wait(barrier, peers)

    own = pl.ds(pl.multiple_of(mine * rows, rows), rows)

    def deal(which, h):
        src = (q_ref, k_ref, v_ref)[which].at[:, pl.ds(h * width, width)]
        dst = (
            qcat.at[head, own, pl.ds(0, width)],
            kcat.at[0, own, pl.ds(0, width)],
            vbuf.at[0, own],
        )[which]
        return src, dst

    for which in range(3):
        for h in range(SIDE):
            target = base + h * SIDE + head
            src, dst = deal(which, h)

            @pl.when(target != me)
            def _():
                pltpu.make_async_remote_copy(
                    src_ref=src,
                    dst_ref=dst,
                    send_sem=deal_send.at[which, h],
                    recv_sem=deal_recv.at[which, mine],
                    device_id={"blk": target},
                    device_id_type=MESH,
                ).start()

            @pl.when(target == me)
            def _():
                pltpu.make_async_copy(src, dst, deal_recv.at[which, mine]).start()

    row_at = lax.broadcasted_iota(jnp.int32, (rows, rows), 0)
    col_at = lax.broadcasted_iota(jnp.int32, (rows, rows), 1)
    eye = row_at == col_at
    power = power_ref[head] * (-LOG2E)
    scale = scale_ref[head]

    def fill_table(at, _):
        distance = (at - (SIDE - 1)) * rows + row_at - col_at
        far = jnp.maximum(distance, 0).astype(jnp.float32)
        table[at] = jnp.where(distance >= 0, power * jnp.log(1.0 + scale * far), NEG)
        return 0

    lax.fori_loop(0, table.shape[0], fill_table, 0)

    ends = []
    for doc in range(lengths_ref.shape[0]):
        ends.append(lengths_ref[doc] + (ends[-1] if ends else 0))
    lane = lax.broadcasted_iota(jnp.int32, (rows, width), 1)
    line = lax.broadcasted_iota(jnp.int32, (rows, width), 0)

    def in_doc(start):
        position = line + start
        doc = jnp.zeros((rows, width), jnp.int32)
        for end in ends:
            doc = doc + (position >= end).astype(jnp.int32)
        return doc == lane

    def fill_query(at, _):
        group, part = at // SIDE, at % SIDE
        same = in_doc(base * rows + at * rows)
        where_to = pl.ds(pl.multiple_of(part * rows, rows), rows)
        qcat[group, where_to, pl.ds(width, width)] = jnp.where(same, 1.0, 0.0).astype(jnp.bfloat16)
        return 0

    def fill_key(at, _):
        back, part = at // SIDE, at % SIDE
        same = in_doc((base - back * CELL + mine * SIDE + part) * rows)
        fill = jnp.where(same | (lane >= len(ends)), 0.0, NEG).astype(jnp.bfloat16)
        where_to = pl.ds(pl.multiple_of(part * rows, rows), rows)
        kcat[back, where_to, pl.ds(width, width)] = fill
        return 0

    lax.fori_loop(0, CELL, fill_query, 0)
    lax.fori_loop(0, 3 * SIDE, fill_key, 0)
    top[...] = jnp.full(top.shape, NEG, jnp.float32)
    tot[...] = jnp.zeros_like(tot)
    acc[...] = jnp.zeros_like(acc)

    def dealt(which):
        for slot in range(SIDE):
            at = pl.ds(slot * rows, rows)
            dst = (
                qcat.at[mine, at, pl.ds(0, width)],
                kcat.at[0, at, pl.ds(0, width)],
                vbuf.at[0, at],
            )[which]
            pltpu.make_async_copy(dst, dst, deal_recv.at[which, slot]).wait()

    def share(step):
        other = lax.rem(mine + step, SIDE)
        block = qcat.at[mine, :, pl.ds(0, width)]
        return pltpu.make_async_remote_copy(
            src_ref=block,
            dst_ref=block,
            send_sem=share_send.at[step],
            recv_sem=share_recv.at[mine],
            device_id={"blk": quarter + other},
            device_id_type=MESH,
        )

    def pass_on(which, hop):
        return pltpu.make_async_remote_copy(
            src_ref=(kcat.at[0, :, pl.ds(0, width)], vbuf.at[0])[which],
            dst_ref=(kcat.at[hop, :, pl.ds(0, width)], vbuf.at[hop])[which],
            send_sem=pass_send.at[which, hop],
            recv_sem=pass_recv.at[which, hop],
            device_id={"blk": me + hop * CELL},
            device_id_type=MESH,
        )

    dealt(0)
    for step in range(1, SIDE):
        share(step).start()
    for which in range(2):
        dealt(which + 1)
        for hop in (1, 2):

            @pl.when(me + hop * CELL < count)
            def _():
                pass_on(which, hop).start()

    to_log2 = LOG2E / math.sqrt(width)

    def attend(m, back, group):
        keys = kcat[back]
        values = vbuf[back]
        for part in range(SIDE):
            at = pl.ds(part * rows, rows)
            scores = lax.dot_general(
                qcat[group, at, :],
                keys,
                (((1,), (1,)), ((), ())),
                preferred_element_type=jnp.float32,
            )
            shifted = [
                scores[:, piece * rows : (piece + 1) * rows] * to_log2
                + table[m * SIDE + part - piece + SIDE - 1]
                for piece in range(SIDE)
            ]
            best = functools.reduce(jnp.maximum, shifted)
            top_old = top[group, at, :]
            top_new = jnp.maximum(top_old, jnp.max(best, axis=1, keepdims=True))
            rescale = jnp.exp2(top_old - top_new)
            weights = [jnp.exp2(piece - top_new) for piece in shifted]
            top[group, at, :] = top_new
            tot[group, at, :] = tot[group, at, :] * rescale + functools.reduce(jnp.add, weights)
            probs = jnp.concatenate([piece.astype(jnp.bfloat16) for piece in weights], axis=1)
            acc[group, at, :] = acc[group, at, :] * rescale[:, :1] + jnp.dot(
                probs, values, preferred_element_type=jnp.float32
            )

    def finished(group, part):
        at = pl.ds(part * rows, rows)
        total = jnp.maximum(jnp.sum(tot[group, at, :], axis=1, keepdims=True), TINY)
        return acc[group, at, :] / total, top[group, at, :] + jnp.log2(total)

    def hand_over(group):
        part = pltpu.make_async_remote_copy(
            src_ref=part_out.at[group],
            dst_ref=part_in.at[mine],
            send_sem=part_send.at[group],
            recv_sem=part_recv.at[mine],
            device_id={"blk": quarter + group},
            device_id_type=MESH,
        )
        stat = pltpu.make_async_remote_copy(
            src_ref=stat_out.at[group],
            dst_ref=stat_in.at[mine],
            send_sem=stat_send.at[group],
            recv_sem=stat_recv.at[mine],
            device_id={"blk": quarter + group},
            device_id_type=MESH,
        )
        return part, stat

    def turn(m, _):
        back = (m + mine) // SIDE
        group = lax.rem(m + mine, SIDE)

        @pl.when((m > 0) & (m < SIDE))
        def _():
            block = qcat.at[group, :, pl.ds(0, width)]
            pltpu.make_async_copy(block, block, share_recv.at[group]).wait()

        @pl.when((m > 0) & (group == 0) & (back <= cell))
        def _():
            block = kcat.at[back, :, pl.ds(0, width)]
            pltpu.make_async_copy(block, block, pass_recv.at[0, back]).wait()
            block = vbuf.at[back]
            pltpu.make_async_copy(block, block, pass_recv.at[1, back]).wait()

        @pl.when(back <= cell)
        def _():
            attend(m, back, group)

        @pl.when((m > SIDE) & (m < 2 * SIDE))
        def _():
            for part in range(SIDE):
                value, level = finished(group, part)
                part_out[group, pl.ds(part * rows, rows), :] = value.astype(jnp.bfloat16)
                stat_out[group, pl.ds(part, 1), :] = jnp.sum(
                    jnp.where(eye, level, 0.0), axis=0, keepdims=True
                )
            for copy in hand_over(group):
                copy.start()

        return 0

    lax.fori_loop(0, 2 * SIDE + 1, turn, 0)

    others = [lax.rem(mine + step, SIDE) for step in range(1, SIDE)]
    for other in others:
        block = part_in.at[other]
        pltpu.make_async_copy(block, block, part_recv.at[other]).wait()
        block = stat_in.at[other]
        pltpu.make_async_copy(block, block, stat_recv.at[other]).wait()

    def home(part):
        src = merged.at[pl.ds(part * rows, rows)]
        dst = out_ref.at[:, pl.ds(pl.multiple_of(head * width, width), width)]
        return src, dst, base + mine * SIDE + part

    def send_home(part):
        src, dst, target = home(part)
        return pltpu.make_async_remote_copy(
            src_ref=src,
            dst_ref=dst,
            send_sem=back_send.at[part],
            recv_sem=back_recv.at[head],
            device_id={"blk": target},
            device_id_type=MESH,
        )

    for part in range(SIDE):
        at = pl.ds(part * rows, rows)
        value, level = finished(mine, part)
        values, levels = [value], [level[:, :1]]
        for other in others:
            values.append(part_in[other, at, :].astype(jnp.float32))
            line_of = stat_in[other, pl.ds(part, 1), :]
            levels.append(jnp.sum(jnp.where(eye, line_of, 0.0), axis=1, keepdims=True))
        most = functools.reduce(jnp.maximum, levels)
        shares = [jnp.exp2(level - most) for level in levels]
        total = functools.reduce(jnp.add, shares)
        whole = functools.reduce(jnp.add, [v * s for v, s in zip(values, shares)]) / total
        merged[at, :] = whole.astype(jnp.bfloat16)
        src, dst, target = home(part)

        @pl.when(target != me)
        def _():
            send_home(part).start()

        @pl.when(target == me)
        def _():
            pltpu.make_async_copy(src, dst, back_recv.at[head]).start()

    for h in range(SIDE):
        block = out_ref.at[:, pl.ds(h * width, width)]
        pltpu.make_async_copy(block, block, back_recv.at[h]).wait()

    for which in range(3):
        for h in range(SIDE):
            src, _ = deal(which, h)

            @pl.when(base + h * SIDE + head != me)
            def _():
                pltpu.make_async_copy(src, src, deal_send.at[which, h]).wait()

    for step in range(1, SIDE):
        share(step).wait_send()
    for which in range(2):
        for hop in (1, 2):

            @pl.when(me + hop * CELL < count)
            def _():
                pass_on(which, hop).wait_send()

    for other in others:
        for copy in hand_over(other):
            copy.wait_send()
    for part in range(SIDE):

        @pl.when(base + mine * SIDE + part != me)
        def _():
            send_home(part).wait_send()


def on_device(query_rows, key_rows, value_rows, kerple_power, kerple_scale, doc_lengths):
    count = lax.axis_size("blk")
    rows, columns = query_rows.shape
    width = columns // SIDE
    span = SIDE * rows
    return pl.pallas_call(
        functools.partial(kernel, rows, width, count),
        out_shape=jax.ShapeDtypeStruct((rows, columns), jnp.bfloat16),
        in_specs=[pl.BlockSpec(memory_space=pltpu.SMEM)] * 3 + [pl.BlockSpec(memory_space=pl.ANY)] * 3,
        out_specs=pl.BlockSpec(memory_space=pl.ANY),
        scratch_shapes=[
            pltpu.VMEM((SIDE, span, 2 * width), jnp.bfloat16),
            pltpu.VMEM((3, span, 2 * width), jnp.bfloat16),
            pltpu.VMEM((3, span, width), jnp.bfloat16),
            pltpu.VMEM((SIDE, span, width), jnp.float32),
            pltpu.VMEM((SIDE, span, rows), jnp.float32),
            pltpu.VMEM((SIDE, span, rows), jnp.float32),
            pltpu.VMEM((2 * CELL + 2 * SIDE - 1, rows, rows), jnp.float32),
            pltpu.VMEM((SIDE, span, width), jnp.bfloat16),
            pltpu.VMEM((SIDE, 2 * SIDE, rows), jnp.float32),
            pltpu.VMEM((SIDE, span, width), jnp.bfloat16),
            pltpu.VMEM((SIDE, 2 * SIDE, rows), jnp.float32),
            pltpu.VMEM((span, width), jnp.bfloat16),
            pltpu.SemaphoreType.DMA((3, SIDE)),
            pltpu.SemaphoreType.DMA((3, SIDE)),
            pltpu.SemaphoreType.DMA((2, 3)),
            pltpu.SemaphoreType.DMA((2, 3)),
            pltpu.SemaphoreType.DMA((SIDE,)),
            pltpu.SemaphoreType.DMA((SIDE,)),
            pltpu.SemaphoreType.DMA((SIDE,)),
            pltpu.SemaphoreType.DMA((SIDE,)),
            pltpu.SemaphoreType.DMA((SIDE,)),
            pltpu.SemaphoreType.DMA((SIDE,)),
            pltpu.SemaphoreType.DMA((SIDE,)),
            pltpu.SemaphoreType.DMA((SIDE,)),
        ],
        compiler_params=pltpu.CompilerParams(
            collective_id=0, has_side_effects=True, vmem_limit_bytes=40 * 2**20
        ),
    )(kerple_power, kerple_scale, doc_lengths, query_rows, key_rows, value_rows)


def solution(mesh):
    block = P(("seq", "blk"), "head")
    return jax.shard_map(
        on_device,
        mesh=mesh,
        in_specs=(block, block, block, P("head"), P("head"), P("seq")),
        out_specs=block,
        check_vma=False,
    )
```

```python
import functools
import math

import jax
import jax.numpy as jnp
from jax import lax
from jax.experimental import pallas as pl
from jax.experimental.pallas import tpu as pltpu
from jax.sharding import PartitionSpec as P

MESH = pl.DeviceIdType.MESH
NEG = -1e30
TINY = 1e-30
SIDE = 4
CELL = SIDE * SIDE
LOG2E = math.log2(math.e)
KEYS, VALUES, QUERIES = 0, 1, 2
STAGES = ((KEYS, VALUES, QUERIES),)


def kernel(
    rows,
    width,
    count,
    power_ref,
    scale_ref,
    lengths_ref,
    q_ref,
    k_ref,
    v_ref,
    out_ref,
    straight,
    turned,
    qcat,
    kcat,
    vbuf,
    shifts,
    acc,
    table,
    part_out,
    stat_out,
    part_in,
    stat_in,
    merged,
    fetch_sem,
    deal_send,
    deal_recv,
    pass_send,
    pass_recv,
    share_send,
    share_recv,
    part_send,
    part_recv,
    stat_send,
    stat_recv,
    back_send,
    back_recv,
):
    me = lax.axis_index("blk")
    cell = me // CELL
    base = cell * CELL
    place = me - base
    head = place // SIDE
    mine = place % SIDE
    quarter = base + head * SIDE
    span = SIDE * rows

    barrier = pltpu.get_barrier_semaphore()
    fetch = pltpu.make_async_copy(v_ref, straight, fetch_sem)
    fetch.start()
    peers = 0
    up, down = me + CELL, me - CELL
    for n in range(SIDE):
        dealt_to, dealt_by, near = base + n * SIDE + head, base + mine * SIDE + n, quarter + n
        for other, meet in (
            (dealt_to, dealt_to != me),
            (dealt_by, (dealt_by != me) & (n != head)),
            (near, (near != me) & (mine != head) & (n != head)),
        ):
            peers = peers + meet.astype(jnp.int32)

            @pl.when(meet)
            def _():
                pl.semaphore_signal(barrier, inc=1, device_id={"blk": other}, device_id_type=MESH)

    for other, meet in (
        (up, up < count),
        (down, down >= 0),
        (up + CELL, up + CELL < count),
        (down - CELL, down >= CELL),
    ):
        peers = peers + meet.astype(jnp.int32)

        @pl.when(meet)
        def _():
            pl.semaphore_signal(barrier, inc=1, device_id={"blk": other}, device_id_type=MESH)

    pl.semaphore_wait(barrier, peers)

    own = pl.ds(pl.multiple_of(mine * rows, rows), rows)

    def deal(which, h):
        columns = pl.ds(h * width, width)
        src = (k_ref.at[:, columns], turned.at[h], q_ref.at[:, columns])[which]
        dst = (
            kcat.at[0, own, pl.ds(0, width)],
            vbuf.at[0, :, own],
            qcat.at[head, own, pl.ds(0, width)],
        )[which]
        return src, dst

    def start_deal(which, h):
        target = base + h * SIDE + head
        src, dst = deal(which, h)

        @pl.when(target != me)
        def _():
            pltpu.make_async_remote_copy(
                src_ref=src,
                dst_ref=dst,
                send_sem=deal_send.at[which, h],
                recv_sem=deal_recv.at[which, mine],
                device_id={"blk": target},
                device_id_type=MESH,
            ).start()

        @pl.when(target == me)
        def _():
            pltpu.make_async_copy(src, dst, deal_recv.at[which, mine]).start()

    def end_deal(which, h):
        src, _ = deal(which, h)

        @pl.when(base + h * SIDE + head != me)
        def _():
            pltpu.make_async_copy(src, src, deal_send.at[which, h]).wait()

    def turn_values():
        fetch.wait()
        for h in range(SIDE):
            block = straight[:, h * width : (h + 1) * width].astype(jnp.float32)
            turned[h] = block.T.astype(jnp.bfloat16)

    if VALUES in STAGES[0]:
        turn_values()
    for which in STAGES[0]:
        for h in range(SIDE):
            start_deal(which, h)

    row_at = lax.broadcasted_iota(jnp.int32, (rows, rows), 0)
    col_at = lax.broadcasted_iota(jnp.int32, (rows, rows), 1)
    power = power_ref[head] * (-LOG2E)
    scale = scale_ref[head]

    def fill_table(at, _):
        distance = (at - (SIDE - 1)) * rows + col_at - row_at
        far = jnp.maximum(distance, 0).astype(jnp.float32)
        table[at] = jnp.where(distance >= 0, power * jnp.log(1.0 + scale * far), NEG)
        return 0

    lax.fori_loop(0, table.shape[0], fill_table, 0)

    ends = []
    for doc in range(lengths_ref.shape[0]):
        ends.append(lengths_ref[doc] + (ends[-1] if ends else 0))
    lane = lax.broadcasted_iota(jnp.int32, (rows, width), 1)
    line = lax.broadcasted_iota(jnp.int32, (rows, width), 0)

    def in_doc(start):
        position = line + start
        doc = jnp.zeros((rows, width), jnp.int32)
        for end in ends:
            doc = doc + (position >= end).astype(jnp.int32)
        return (doc == lane) & (position >= 0)

    def fill_query(at, _):
        group, part = at // SIDE, at % SIDE
        same = in_doc(base * rows + at * rows)
        where_to = pl.ds(pl.multiple_of(part * rows, rows), rows)
        qcat[group, where_to, pl.ds(width, width)] = jnp.where(same, 1.0, 0.0).astype(jnp.bfloat16)
        return 0

    def fill_key(at, _):
        back, part = at // SIDE, at % SIDE
        same = in_doc((base - back * CELL + mine * SIDE + part) * rows)
        fill = jnp.where(same | (lane >= len(ends)), 0.0, NEG).astype(jnp.bfloat16)
        where_to = pl.ds(pl.multiple_of(part * rows, rows), rows)
        kcat[back, where_to, pl.ds(width, width)] = fill
        return 0

    lax.fori_loop(0, CELL, fill_query, 0)
    lax.fori_loop(0, 3 * SIDE, fill_key, 0)

    def blank(back, _):
        kcat[back, :, pl.ds(0, width)] = jnp.zeros((span, width), jnp.bfloat16)
        vbuf[back] = jnp.zeros((width, span), jnp.bfloat16)
        return 0

    lax.fori_loop(jnp.minimum(cell + 1, 3), 3, blank, 0)
    if VALUES not in STAGES[0]:
        turn_values()

    def held(which, back, slot):
        at = pl.ds(slot * rows, rows)
        return (kcat.at[back, at, pl.ds(0, width)], vbuf.at[back, :, at])[which]

    def dealt(which, slot):
        if which == QUERIES:
            block = qcat.at[mine, pl.ds(slot * rows, rows), pl.ds(0, width)]
        else:
            block = held(which, 0, slot)
        pltpu.make_async_copy(block, block, deal_recv.at[which, slot]).wait()

    def pass_on(which, back, slot):
        return pltpu.make_async_remote_copy(
            src_ref=held(which, 0, slot),
            dst_ref=held(which, back, slot),
            send_sem=pass_send.at[which, back - 1, slot],
            recv_sem=pass_recv.at[which, back - 1, slot],
            device_id={"blk": me + back * CELL},
            device_id_type=MESH,
        )

    def first_passes(which):
        for slot in range(SIDE):
            dealt(which, slot)
            for back in (1, 2):

                @pl.when(me + back * CELL < count)
                def _():
                    pass_on(which, back, slot).start()

    def passed(which):
        for back in (1, 2):

            @pl.when(cell >= back)
            def _():
                for slot in range(SIDE):
                    block = held(which, back, slot)
                    pltpu.make_async_copy(block, block, pass_recv.at[which, back - 1, slot]).wait()

    def share(step):
        other = lax.rem(mine + step, SIDE)
        block = qcat.at[mine, :, pl.ds(0, width)]
        return pltpu.make_async_remote_copy(
            src_ref=block,
            dst_ref=block,
            send_sem=share_send.at[step],
            recv_sem=share_recv.at[mine],
            device_id={"blk": quarter + other},
            device_id_type=MESH,
        )

    waited = []
    for number, stage in enumerate(STAGES):
        for which in stage:
            for h in range(SIDE):
                if number + 1 < len(STAGES):
                    end_deal(which, h)
                    waited.append((which, h))
                if number + 1 < len(STAGES) and which == stage[-1]:
                    for later in STAGES[number + 1]:
                        start_deal(later, h)
        for which in stage:
            if which == QUERIES:
                for slot in range(SIDE):
                    dealt(which, slot)
                for step in range(1, SIDE):
                    share(step).start()
            else:
                first_passes(which)
    passed(KEYS)
    passed(VALUES)

    to_log2 = LOG2E / math.sqrt(width)

    def fold(combine, tile):
        return functools.reduce(combine, [tile[at : at + 8] for at in range(0, rows, 8)])

    def attend(first, pairs):
        group = lax.rem(first + mine, SIDE)
        best = [jnp.full((8, rows), 2 * NEG, jnp.float32)] * SIDE
        for pair in range(pairs):
            m = first + pair * SIDE
            scores = lax.dot_general(
                kcat[(m + mine) // SIDE],
                qcat[group],
                (((1,), (1,)), ((), ())),
                preferred_element_type=jnp.float32,
            )
            for part in range(SIDE):
                for piece in range(SIDE):
                    shifted = (
                        scores[piece * rows : (piece + 1) * rows, part * rows : (part + 1) * rows]
                        * to_log2
                        + table[m * SIDE + part - piece + SIDE - 1]
                    )
                    shifts[pair, pl.ds(piece * rows, rows), pl.ds(part * rows, rows)] = shifted
                    best[part] = jnp.maximum(best[part], fold(jnp.maximum, shifted))
        tops = [jnp.max(tile, axis=0, keepdims=True) for tile in best]
        totals = [jnp.zeros((8, rows), jnp.float32)] * SIDE
        for pair in range(pairs):
            m = first + pair * SIDE
            probs = []
            for part in range(SIDE):
                weights = []
                for piece in range(SIDE):
                    shifted = shifts[pair, pl.ds(piece * rows, rows), pl.ds(part * rows, rows)]
                    weight = jnp.exp2(shifted - tops[part])
                    totals[part] = totals[part] + fold(jnp.add, weight)
                    weights.append(weight.astype(jnp.bfloat16))
                probs.append(jnp.concatenate(weights, axis=0))
            product = jnp.dot(
                vbuf[(m + mine) // SIDE],
                jnp.concatenate(probs, axis=1),
                preferred_element_type=jnp.float32,
            )
            acc[...] = product if pair == 0 else acc[...] + product
        for part in range(SIDE):
            total = jnp.sum(totals[part], axis=0, keepdims=True)
            level = tops[part] + jnp.log2(total)
            at = pl.ds(part * rows, rows)
            part_out[group, :, at] = (acc[:, at] / total).astype(jnp.bfloat16)
            stat_out[group, pl.ds(part, 1), :] = level

    def hand_over(group):
        part = pltpu.make_async_remote_copy(
            src_ref=part_out.at[group],
            dst_ref=part_in.at[mine],
            send_sem=part_send.at[group],
            recv_sem=part_recv.at[mine],
            device_id={"blk": quarter + group},
            device_id_type=MESH,
        )
        stat = pltpu.make_async_remote_copy(
            src_ref=stat_out.at[group],
            dst_ref=stat_in.at[mine],
            send_sem=stat_send.at[group],
            recv_sem=stat_recv.at[mine],
            device_id={"blk": quarter + group},
            device_id_type=MESH,
        )
        return part, stat

    attend(0, 3)

    def turn(first, _):
        group = lax.rem(first + mine, SIDE)
        block = qcat.at[group, :, pl.ds(0, width)]
        pltpu.make_async_copy(block, block, share_recv.at[group]).wait()
        attend(first, 2)
        for copy in hand_over(group):
            copy.start()
        return 0

    lax.fori_loop(1, SIDE, turn, 0)

    others = [lax.rem(mine + step, SIDE) for step in range(1, SIDE)]
    for other in others:
        block = part_in.at[other]
        pltpu.make_async_copy(block, block, part_recv.at[other]).wait()
        block = stat_in.at[other]
        pltpu.make_async_copy(block, block, stat_recv.at[other]).wait()

    def home(part):
        src = merged.at[pl.ds(part * rows, rows)]
        dst = out_ref.at[:, pl.ds(pl.multiple_of(head * width, width), width)]
        return src, dst, base + mine * SIDE + part

    def send_home(part):
        src, dst, target = home(part)
        return pltpu.make_async_remote_copy(
            src_ref=src,
            dst_ref=dst,
            send_sem=back_send.at[part],
            recv_sem=back_recv.at[head],
            device_id={"blk": target},
            device_id_type=MESH,
        )

    for part in range(SIDE):
        at = pl.ds(part * rows, rows)
        values = [part_out[mine, :, at]] + [part_in[other, :, at] for other in others]
        levels = [stat_out[mine, pl.ds(part, 1), :]]
        levels += [stat_in[other, pl.ds(part, 1), :] for other in others]
        most = functools.reduce(jnp.maximum, levels)
        shares = [jnp.exp2(level - most) for level in levels]
        total = functools.reduce(jnp.add, shares)
        whole = [v.astype(jnp.float32) * s for v, s in zip(values, shares)]
        whole = functools.reduce(jnp.add, whole) / total
        merged[at, :] = whole.T.astype(jnp.bfloat16)
        src, dst, target = home(part)

        @pl.when(target != me)
        def _():
            send_home(part).start()

        @pl.when(target == me)
        def _():
            pltpu.make_async_copy(src, dst, back_recv.at[head]).start()

    for h in range(SIDE):
        block = out_ref.at[:, pl.ds(h * width, width)]
        pltpu.make_async_copy(block, block, back_recv.at[h]).wait()

    for which in range(3):
        for h in range(SIDE):
            if (which, h) not in waited:
                end_deal(which, h)
    for step in range(1, SIDE):
        share(step).wait_send()
    for which in (KEYS, VALUES):
        for back in (1, 2):

            @pl.when(me + back * CELL < count)
            def _():
                for slot in range(SIDE):
                    pass_on(which, back, slot).wait_send()

    for other in others:
        for copy in hand_over(other):
            copy.wait_send()
    for part in range(SIDE):

        @pl.when(base + mine * SIDE + part != me)
        def _():
            send_home(part).wait_send()


def on_device(query_rows, key_rows, value_rows, kerple_power, kerple_scale, doc_lengths):
    count = lax.axis_size("blk")
    rows, columns = query_rows.shape
    width = columns // SIDE
    span = SIDE * rows
    return pl.pallas_call(
        functools.partial(kernel, rows, width, count),
        out_shape=jax.ShapeDtypeStruct((rows, columns), jnp.bfloat16),
        in_specs=[pl.BlockSpec(memory_space=pltpu.SMEM)] * 3 + [pl.BlockSpec(memory_space=pl.ANY)] * 3,
        out_specs=pl.BlockSpec(memory_space=pl.ANY),
        scratch_shapes=[
            pltpu.VMEM((rows, columns), jnp.bfloat16),
            pltpu.VMEM((SIDE, width, rows), jnp.bfloat16),
            pltpu.VMEM((SIDE, span, 2 * width), jnp.bfloat16),
            pltpu.VMEM((3, span, 2 * width), jnp.bfloat16),
            pltpu.VMEM((3, width, span), jnp.bfloat16),
            pltpu.VMEM((3, span, span), jnp.float32),
            pltpu.VMEM((width, span), jnp.float32),
            pltpu.VMEM((2 * CELL + 2 * SIDE - 1, rows, rows), jnp.float32),
            pltpu.VMEM((SIDE, width, span), jnp.bfloat16),
            pltpu.VMEM((SIDE, 2 * SIDE, rows), jnp.float32),
            pltpu.VMEM((SIDE, width, span), jnp.bfloat16),
            pltpu.VMEM((SIDE, 2 * SIDE, rows), jnp.float32),
            pltpu.VMEM((span, width), jnp.bfloat16),
            pltpu.SemaphoreType.DMA,
            pltpu.SemaphoreType.DMA((3, SIDE)),
            pltpu.SemaphoreType.DMA((3, SIDE)),
            pltpu.SemaphoreType.DMA((2, 2, SIDE)),
            pltpu.SemaphoreType.DMA((2, 2, SIDE)),
            pltpu.SemaphoreType.DMA((SIDE,)),
            pltpu.SemaphoreType.DMA((SIDE,)),
            pltpu.SemaphoreType.DMA((SIDE,)),
            pltpu.SemaphoreType.DMA((SIDE,)),
            pltpu.SemaphoreType.DMA((SIDE,)),
            pltpu.SemaphoreType.DMA((SIDE,)),
            pltpu.SemaphoreType.DMA((SIDE,)),
            pltpu.SemaphoreType.DMA((SIDE,)),
        ],
        compiler_params=pltpu.CompilerParams(
            collective_id=0, has_side_effects=True, vmem_limit_bytes=60 * 2**20
        ),
    )(kerple_power, kerple_scale, doc_lengths, query_rows, key_rows, value_rows)


def solution(mesh):
    block = P(("seq", "blk"), "head")
    return jax.shard_map(
        on_device,
        mesh=mesh,
        in_specs=(block, block, block, P("head"), P("head"), P("seq")),
        out_specs=block,
        check_vma=False,
    )
```

```python
import functools
import math

import jax
import jax.numpy as jnp
from jax import lax
from jax.experimental import pallas as pl
from jax.experimental.pallas import tpu as pltpu
from jax.sharding import PartitionSpec as P

MESH = pl.DeviceIdType.MESH
NEG = -1e30
TINY = 1e-30
SIDE = 4
CELL = SIDE * SIDE
LOG2E = math.log2(math.e)
KEYS, VALUES, QUERIES = 0, 1, 2
EARLY, LATE = (KEYS, QUERIES), (VALUES,)


def kernel(
    rows,
    width,
    count,
    power_ref,
    scale_ref,
    lengths_ref,
    q_ref,
    k_ref,
    v_ref,
    out_ref,
    straight,
    turned,
    qcat,
    kcat,
    vbuf,
    shifts,
    acc,
    table,
    part_out,
    stat_out,
    part_in,
    stat_in,
    kept,
    merged,
    fetch_sem,
    deal_send,
    deal_recv,
    pass_send,
    pass_recv,
    share_send,
    share_recv,
    part_send,
    part_recv,
    stat_send,
    stat_recv,
    back_send,
    back_recv,
):
    me = lax.axis_index("blk")
    cell = me // CELL
    base = cell * CELL
    place = me - base
    head = place // SIDE
    mine = place % SIDE
    quarter = base + head * SIDE
    span = SIDE * rows

    barrier = pltpu.get_barrier_semaphore()
    fetch = pltpu.make_async_copy(v_ref, straight, fetch_sem)
    fetch.start()
    peers = 0
    up, down = me + CELL, me - CELL
    for n in range(SIDE):
        dealt_to, dealt_by, near = base + n * SIDE + head, base + mine * SIDE + n, quarter + n
        for other, meet in (
            (dealt_to, dealt_to != me),
            (dealt_by, (dealt_by != me) & (n != head)),
            (near, (near != me) & (mine != head) & (n != head)),
        ):
            peers = peers + meet.astype(jnp.int32)

            @pl.when(meet)
            def _():
                pl.semaphore_signal(barrier, inc=1, device_id={"blk": other}, device_id_type=MESH)

    for other, meet in (
        (up, up < count),
        (down, down >= 0),
        (up + CELL, up + CELL < count),
        (down - CELL, down >= CELL),
    ):
        peers = peers + meet.astype(jnp.int32)

        @pl.when(meet)
        def _():
            pl.semaphore_signal(barrier, inc=1, device_id={"blk": other}, device_id_type=MESH)

    pl.semaphore_wait(barrier, peers)

    own = pl.ds(pl.multiple_of(mine * rows, rows), rows)

    def deal(which, h):
        columns = pl.ds(h * width, width)
        src = (k_ref.at[:, columns], turned.at[h], q_ref.at[:, columns])[which]
        dst = (
            kcat.at[0, own, pl.ds(0, width)],
            vbuf.at[0, :, own],
            qcat.at[head, own, pl.ds(0, width)],
        )[which]
        return src, dst

    def start_deal(which, h):
        target = base + h * SIDE + head
        src, dst = deal(which, h)

        @pl.when(target != me)
        def _():
            pltpu.make_async_remote_copy(
                src_ref=src,
                dst_ref=dst,
                send_sem=deal_send.at[which, h],
                recv_sem=deal_recv.at[which, mine],
                device_id={"blk": target},
                device_id_type=MESH,
            ).start()

        @pl.when(target == me)
        def _():
            pltpu.make_async_copy(src, dst, deal_recv.at[which, mine]).start()

    def end_deal(which, h):
        src, _ = deal(which, h)

        @pl.when(base + h * SIDE + head != me)
        def _():
            pltpu.make_async_copy(src, src, deal_send.at[which, h]).wait()

    def turn_values():
        fetch.wait()
        for h in range(SIDE):
            block = straight[:, h * width : (h + 1) * width].astype(jnp.float32)
            turned[h] = block.T.astype(jnp.bfloat16)

    for which in EARLY:
        if which == VALUES:
            turn_values()
        for h in range(SIDE):
            start_deal(which, h)

    row_at = lax.broadcasted_iota(jnp.int32, (rows, rows), 0)
    col_at = lax.broadcasted_iota(jnp.int32, (rows, rows), 1)
    power = power_ref[head] * (-LOG2E)
    scale = scale_ref[head]

    def fill_table(at, _):
        distance = (at - (SIDE - 1)) * rows + col_at - row_at
        far = jnp.maximum(distance, 0).astype(jnp.float32)
        table[at] = jnp.where(distance >= 0, power * jnp.log(1.0 + scale * far), NEG)
        return 0

    lax.fori_loop(0, table.shape[0], fill_table, 0)

    ends = []
    for doc in range(lengths_ref.shape[0]):
        ends.append(lengths_ref[doc] + (ends[-1] if ends else 0))
    lane = lax.broadcasted_iota(jnp.int32, (rows, width), 1)
    line = lax.broadcasted_iota(jnp.int32, (rows, width), 0)

    def in_doc(start):
        position = line + start
        doc = jnp.zeros((rows, width), jnp.int32)
        for end in ends:
            doc = doc + (position >= end).astype(jnp.int32)
        return (doc == lane) & (position >= 0)

    def fill_query(at, _):
        group, part = at // SIDE, at % SIDE
        same = in_doc(base * rows + at * rows)
        where_to = pl.ds(pl.multiple_of(part * rows, rows), rows)
        qcat[group, where_to, pl.ds(width, width)] = jnp.where(same, 1.0, 0.0).astype(jnp.bfloat16)
        return 0

    def fill_key(at, _):
        back, part = at // SIDE, at % SIDE
        same = in_doc((base - back * CELL + mine * SIDE + part) * rows)
        fill = jnp.where(same | (lane >= len(ends)), 0.0, NEG).astype(jnp.bfloat16)
        where_to = pl.ds(pl.multiple_of(part * rows, rows), rows)
        kcat[back, where_to, pl.ds(width, width)] = fill
        return 0

    lax.fori_loop(0, CELL, fill_query, 0)
    lax.fori_loop(0, 3 * SIDE, fill_key, 0)

    def blank(back, _):
        kcat[back, :, pl.ds(0, width)] = jnp.zeros((span, width), jnp.bfloat16)
        vbuf[back] = jnp.zeros((width, span), jnp.bfloat16)
        return 0

    lax.fori_loop(jnp.minimum(cell + 1, 3), 3, blank, 0)
    for which in LATE:
        if which == VALUES:
            turn_values()
        for h in range(SIDE):
            start_deal(which, h)

    def held(which, back, slot):
        at = pl.ds(slot * rows, rows)
        return (kcat.at[back, at, pl.ds(0, width)], vbuf.at[back, :, at])[which]

    def dealt(which, slot):
        if which == QUERIES:
            block = qcat.at[mine, pl.ds(slot * rows, rows), pl.ds(0, width)]
        else:
            block = held(which, 0, slot)
        pltpu.make_async_copy(block, block, deal_recv.at[which, slot]).wait()

    def pass_on(which, back, slot):
        return pltpu.make_async_remote_copy(
            src_ref=held(which, 0, slot),
            dst_ref=held(which, back, slot),
            send_sem=pass_send.at[which, back - 1, slot],
            recv_sem=pass_recv.at[which, back - 1, slot],
            device_id={"blk": me + back * CELL},
            device_id_type=MESH,
        )

    def first_passes(which):
        for slot in range(SIDE):
            dealt(which, slot)
            for back in (1, 2):

                @pl.when(me + back * CELL < count)
                def _():
                    pass_on(which, back, slot).start()

    def passed(which):
        for back in (1, 2):

            @pl.when(cell >= back)
            def _():
                for slot in range(SIDE):
                    block = held(which, back, slot)
                    pltpu.make_async_copy(block, block, pass_recv.at[which, back - 1, slot]).wait()

    beside = mine + 1 - 2 * lax.rem(mine, 2)
    across = mine + 2 - 4 * (mine // 2)
    diagonal = SIDE - 1 - mine

    def share(group, to):
        block = qcat.at[group, :, pl.ds(0, width)]
        return pltpu.make_async_remote_copy(
            src_ref=block,
            dst_ref=block,
            send_sem=share_send.at[to],
            recv_sem=share_recv.at[group],
            device_id={"blk": quarter + to},
            device_id_type=MESH,
        )

    def shared(group):
        block = qcat.at[group, :, pl.ds(0, width)]
        pltpu.make_async_copy(block, block, share_recv.at[group]).wait()

    def share_own():
        for slot in range(SIDE):
            dealt(QUERIES, slot)
        share(mine, across).start()
        share(mine, beside).start()

    first_passes(KEYS)
    share_own()
    first_passes(VALUES)
    shared(across)
    hand_on = pltpu.make_async_remote_copy(
        src_ref=qcat.at[across, :, pl.ds(0, width)],
        dst_ref=qcat.at[across, :, pl.ds(0, width)],
        send_sem=share_send.at[diagonal],
        recv_sem=share_recv.at[across],
        device_id={"blk": quarter + beside},
        device_id_type=MESH,
    )
    hand_on.start()
    passed(KEYS)
    passed(VALUES)

    to_log2 = LOG2E / math.sqrt(width)

    def fold(combine, tile):
        return functools.reduce(combine, [tile[at : at + 8] for at in range(0, rows, 8)])

    def attend(first, pairs):
        group = mine if pairs == 3 else lax.rem(first + mine, SIDE)
        best = [jnp.full((8, rows), 2 * NEG, jnp.float32)] * SIDE
        for pair in range(pairs):
            m = first + pair * SIDE
            scores = lax.dot_general(
                kcat[(m + mine) // SIDE],
                qcat[group],
                (((1,), (1,)), ((), ())),
                preferred_element_type=jnp.float32,
            )
            for part in range(SIDE):
                for piece in range(SIDE):
                    shifted = (
                        scores[piece * rows : (piece + 1) * rows, part * rows : (part + 1) * rows]
                        * to_log2
                        + table[m * SIDE + part - piece + SIDE - 1]
                    )
                    shifts[pair, pl.ds(piece * rows, rows), pl.ds(part * rows, rows)] = shifted
                    best[part] = jnp.maximum(best[part], fold(jnp.maximum, shifted))
        tops = [jnp.max(tile, axis=0, keepdims=True) for tile in best]
        totals = [jnp.zeros((8, rows), jnp.float32)] * SIDE
        for pair in range(pairs):
            m = first + pair * SIDE
            probs = []
            for part in range(SIDE):
                weights = []
                for piece in range(SIDE):
                    shifted = shifts[pair, pl.ds(piece * rows, rows), pl.ds(part * rows, rows)]
                    weight = jnp.exp2(shifted - tops[part])
                    totals[part] = totals[part] + fold(jnp.add, weight)
                    weights.append(weight.astype(jnp.bfloat16))
                probs.append(jnp.concatenate(weights, axis=0))
            product = jnp.dot(
                vbuf[(m + mine) // SIDE],
                jnp.concatenate(probs, axis=1),
                preferred_element_type=jnp.float32,
            )
            acc[...] = product if pair == 0 else acc[...] + product
        for part in range(SIDE):
            total = jnp.sum(totals[part], axis=0, keepdims=True)
            level = tops[part] + jnp.log2(total)
            at = pl.ds(part * rows, rows)
            if pairs == 3:
                kept[:, at] = acc[:, at] / total
            else:
                part_out[group, :, at] = (acc[:, at] / total).astype(jnp.bfloat16)
            stat_out[group, pl.ds(part, 1), :] = level

    def hand_over(group):
        part = pltpu.make_async_remote_copy(
            src_ref=part_out.at[group],
            dst_ref=part_in.at[mine],
            send_sem=part_send.at[group],
            recv_sem=part_recv.at[mine],
            device_id={"blk": quarter + group},
            device_id_type=MESH,
        )
        stat = pltpu.make_async_remote_copy(
            src_ref=stat_out.at[group],
            dst_ref=stat_in.at[mine],
            send_sem=stat_send.at[group],
            recv_sem=stat_recv.at[mine],
            device_id={"blk": quarter + group},
            device_id_type=MESH,
        )
        return part, stat

    def turn(group, _):
        @pl.when(group == mine)
        def _():
            attend(0, 3)

        @pl.when(group != mine)
        def _():
            @pl.when(group != across)
            def _():
                shared(group)

            attend(lax.rem(group - mine + SIDE, SIDE), 2)
            for copy in hand_over(group):
                copy.start()

        return 0

    lax.fori_loop(0, SIDE, turn, 0)

    others = [lax.rem(mine + step, SIDE) for step in range(1, SIDE)]
    for other in others:
        block = part_in.at[other]
        pltpu.make_async_copy(block, block, part_recv.at[other]).wait()
        block = stat_in.at[other]
        pltpu.make_async_copy(block, block, stat_recv.at[other]).wait()

    def home(part):
        src = merged.at[pl.ds(part * rows, rows)]
        dst = out_ref.at[:, pl.ds(pl.multiple_of(head * width, width), width)]
        return src, dst, base + mine * SIDE + part

    def send_home(part):
        src, dst, target = home(part)
        return pltpu.make_async_remote_copy(
            src_ref=src,
            dst_ref=dst,
            send_sem=back_send.at[part],
            recv_sem=back_recv.at[head],
            device_id={"blk": target},
            device_id_type=MESH,
        )

    for part in range(SIDE):
        at = pl.ds(part * rows, rows)
        values = [kept[:, at]] + [part_in[other, :, at] for other in others]
        levels = [stat_out[mine, pl.ds(part, 1), :]]
        levels += [stat_in[other, pl.ds(part, 1), :] for other in others]
        most = functools.reduce(jnp.maximum, levels)
        shares = [jnp.exp2(level - most) for level in levels]
        total = functools.reduce(jnp.add, shares)
        whole = [v.astype(jnp.float32) * s for v, s in zip(values, shares)]
        whole = functools.reduce(jnp.add, whole) / total
        merged[at, :] = whole.T.astype(jnp.bfloat16)
        src, dst, target = home(part)

        @pl.when(target != me)
        def _():
            send_home(part).start()

        @pl.when(target == me)
        def _():
            pltpu.make_async_copy(src, dst, back_recv.at[head]).start()

    for h in range(SIDE):
        block = out_ref.at[:, pl.ds(h * width, width)]
        pltpu.make_async_copy(block, block, back_recv.at[h]).wait()

    for which in range(3):
        for h in range(SIDE):
            end_deal(which, h)
    share(mine, across).wait_send()
    share(mine, beside).wait_send()
    hand_on.wait_send()
    for which in (KEYS, VALUES):
        for back in (1, 2):

            @pl.when(me + back * CELL < count)
            def _():
                for slot in range(SIDE):
                    pass_on(which, back, slot).wait_send()

    for other in others:
        for copy in hand_over(other):
            copy.wait_send()
    for part in range(SIDE):

        @pl.when(base + mine * SIDE + part != me)
        def _():
            send_home(part).wait_send()


def on_device(query_rows, key_rows, value_rows, kerple_power, kerple_scale, doc_lengths):
    count = lax.axis_size("blk")
    rows, columns = query_rows.shape
    width = columns // SIDE
    span = SIDE * rows
    return pl.pallas_call(
        functools.partial(kernel, rows, width, count),
        out_shape=jax.ShapeDtypeStruct((rows, columns), jnp.bfloat16),
        in_specs=[pl.BlockSpec(memory_space=pltpu.SMEM)] * 3 + [pl.BlockSpec(memory_space=pl.ANY)] * 3,
        out_specs=pl.BlockSpec(memory_space=pl.ANY),
        scratch_shapes=[
            pltpu.VMEM((rows, columns), jnp.bfloat16),
            pltpu.VMEM((SIDE, width, rows), jnp.bfloat16),
            pltpu.VMEM((SIDE, span, 2 * width), jnp.bfloat16),
            pltpu.VMEM((3, span, 2 * width), jnp.bfloat16),
            pltpu.VMEM((3, width, span), jnp.bfloat16),
            pltpu.VMEM((3, span, span), jnp.float32),
            pltpu.VMEM((width, span), jnp.float32),
            pltpu.VMEM((2 * CELL + 2 * SIDE - 1, rows, rows), jnp.float32),
            pltpu.VMEM((SIDE, width, span), jnp.bfloat16),
            pltpu.VMEM((SIDE, 2 * SIDE, rows), jnp.float32),
            pltpu.VMEM((SIDE, width, span), jnp.bfloat16),
            pltpu.VMEM((SIDE, 2 * SIDE, rows), jnp.float32),
            pltpu.VMEM((width, span), jnp.float32),
            pltpu.VMEM((span, width), jnp.bfloat16),
            pltpu.SemaphoreType.DMA,
            pltpu.SemaphoreType.DMA((3, SIDE)),
            pltpu.SemaphoreType.DMA((3, SIDE)),
            pltpu.SemaphoreType.DMA((2, 2, SIDE)),
            pltpu.SemaphoreType.DMA((2, 2, SIDE)),
            pltpu.SemaphoreType.DMA((SIDE,)),
            pltpu.SemaphoreType.DMA((SIDE,)),
            pltpu.SemaphoreType.DMA((SIDE,)),
            pltpu.SemaphoreType.DMA((SIDE,)),
            pltpu.SemaphoreType.DMA((SIDE,)),
            pltpu.SemaphoreType.DMA((SIDE,)),
            pltpu.SemaphoreType.DMA((SIDE,)),
            pltpu.SemaphoreType.DMA((SIDE,)),
        ],
        compiler_params=pltpu.CompilerParams(
            collective_id=0, has_side_effects=True, vmem_limit_bytes=60 * 2**20
        ),
    )(kerple_power, kerple_scale, doc_lengths, query_rows, key_rows, value_rows)


def solution(mesh):
    block = P(("seq", "blk"), "head")
    return jax.shard_map(
        on_device,
        mesh=mesh,
        in_specs=(block, block, block, P("head"), P("head"), P("seq")),
        out_specs=block,
        check_vma=False,
    )
```

```python
import functools
import math

import jax
import jax.numpy as jnp
from jax import lax
from jax.experimental import pallas as pl
from jax.experimental.pallas import tpu as pltpu
from jax.sharding import PartitionSpec as P

MESH = pl.DeviceIdType.MESH
NEG = -1e30
TINY = 1e-30
SIDE = 4
CELL = SIDE * SIDE
LOG2E = math.log2(math.e)
KEYS, VALUES, QUERIES = 0, 1, 2
EARLY, LATE = (KEYS, QUERIES), (VALUES,)


def kernel(
    rows,
    width,
    count,
    power_ref,
    scale_ref,
    lengths_ref,
    q_ref,
    k_ref,
    v_ref,
    out_ref,
    k_here,
    q_here,
    straight,
    turned,
    qcat,
    kcat,
    vbuf,
    shifts,
    acc,
    table,
    part_out,
    stat_out,
    part_in,
    stat_in,
    kept,
    merged,
    fetch_sem,
    deal_send,
    deal_recv,
    pass_send,
    pass_recv,
    share_send,
    share_recv,
    part_send,
    part_recv,
    stat_send,
    stat_recv,
    back_send,
    back_recv,
):
    me = lax.axis_index("blk")
    cell = me // CELL
    base = cell * CELL
    place = me - base
    head = place // SIDE
    mine = place % SIDE
    quarter = base + head * SIDE
    span = SIDE * rows

    barrier = pltpu.get_barrier_semaphore()
    fetch = pltpu.make_async_copy(v_ref, straight, fetch_sem.at[0])
    near_k = pltpu.make_async_copy(k_ref, k_here, fetch_sem.at[1])
    near_q = pltpu.make_async_copy(q_ref, q_here, fetch_sem.at[2])
    near_k.start()
    near_q.start()
    fetch.start()
    peers = 0
    up, down = me + CELL, me - CELL
    for n in range(SIDE):
        dealt_to, dealt_by, near = base + n * SIDE + head, base + mine * SIDE + n, quarter + n
        for other, meet in (
            (dealt_to, dealt_to != me),
            (dealt_by, (dealt_by != me) & (n != head)),
            (near, (near != me) & (mine != head) & (n != head)),
        ):
            peers = peers + meet.astype(jnp.int32)

            @pl.when(meet)
            def _():
                pl.semaphore_signal(barrier, inc=1, device_id={"blk": other}, device_id_type=MESH)

    for other, meet in (
        (up, up < count),
        (down, down >= 0),
        (up + CELL, up + CELL < count),
        (down - CELL, down >= CELL),
    ):
        peers = peers + meet.astype(jnp.int32)

        @pl.when(meet)
        def _():
            pl.semaphore_signal(barrier, inc=1, device_id={"blk": other}, device_id_type=MESH)

    near_k.wait()
    near_q.wait()
    pl.semaphore_wait(barrier, peers)

    own = pl.ds(pl.multiple_of(mine * rows, rows), rows)

    def deal(which, h):
        columns = pl.ds(h * width, width)
        src = (k_here.at[:, columns], turned.at[h], q_here.at[:, columns])[which]
        dst = (
            kcat.at[0, own, pl.ds(0, width)],
            vbuf.at[0, :, own],
            qcat.at[head, own, pl.ds(0, width)],
        )[which]
        return src, dst

    def start_deal(which, h):
        target = base + h * SIDE + head
        src, dst = deal(which, h)

        @pl.when(target != me)
        def _():
            pltpu.make_async_remote_copy(
                src_ref=src,
                dst_ref=dst,
                send_sem=deal_send.at[which, h],
                recv_sem=deal_recv.at[which, mine],
                device_id={"blk": target},
                device_id_type=MESH,
            ).start()

        @pl.when(target == me)
        def _():
            pltpu.make_async_copy(src, dst, deal_recv.at[which, mine]).start()

    def end_deal(which, h):
        src, _ = deal(which, h)

        @pl.when(base + h * SIDE + head != me)
        def _():
            pltpu.make_async_copy(src, src, deal_send.at[which, h]).wait()

    def turn_values():
        fetch.wait()
        for h in range(SIDE):
            block = straight[:, h * width : (h + 1) * width].astype(jnp.float32)
            turned[h] = block.T.astype(jnp.bfloat16)

    for which in EARLY:
        if which == VALUES:
            turn_values()
        for h in range(SIDE):
            start_deal(which, h)

    row_at = lax.broadcasted_iota(jnp.int32, (rows, rows), 0)
    col_at = lax.broadcasted_iota(jnp.int32, (rows, rows), 1)
    power = power_ref[head] * (-LOG2E)
    scale = scale_ref[head]

    def fill_table(at, _):
        distance = (at - (SIDE - 1)) * rows + col_at - row_at
        far = jnp.maximum(distance, 0).astype(jnp.float32)
        table[at] = jnp.where(distance >= 0, power * jnp.log(1.0 + scale * far), NEG)
        return 0

    lax.fori_loop(0, table.shape[0], fill_table, 0)

    ends = []
    for doc in range(lengths_ref.shape[0]):
        ends.append(lengths_ref[doc] + (ends[-1] if ends else 0))
    lane = lax.broadcasted_iota(jnp.int32, (rows, width), 1)
    line = lax.broadcasted_iota(jnp.int32, (rows, width), 0)

    def in_doc(start):
        position = line + start
        doc = jnp.zeros((rows, width), jnp.int32)
        for end in ends:
            doc = doc + (position >= end).astype(jnp.int32)
        return (doc == lane) & (position >= 0)

    def fill_query(at, _):
        group, part = at // SIDE, at % SIDE
        same = in_doc(base * rows + at * rows)
        where_to = pl.ds(pl.multiple_of(part * rows, rows), rows)
        qcat[group, where_to, pl.ds(width, width)] = jnp.where(same, 1.0, 0.0).astype(jnp.bfloat16)
        return 0

    def fill_key(at, _):
        back, part = at // SIDE, at % SIDE
        same = in_doc((base - back * CELL + mine * SIDE + part) * rows)
        fill = jnp.where(same | (lane >= len(ends)), 0.0, NEG).astype(jnp.bfloat16)
        where_to = pl.ds(pl.multiple_of(part * rows, rows), rows)
        kcat[back, where_to, pl.ds(width, width)] = fill
        return 0

    lax.fori_loop(0, CELL, fill_query, 0)
    lax.fori_loop(0, 3 * SIDE, fill_key, 0)

    def blank(back, _):
        kcat[back, :, pl.ds(0, width)] = jnp.zeros((span, width), jnp.bfloat16)
        vbuf[back] = jnp.zeros((width, span), jnp.bfloat16)
        return 0

    lax.fori_loop(jnp.minimum(cell + 1, 3), 3, blank, 0)
    for which in LATE:
        if which == VALUES:
            turn_values()
        for h in range(SIDE):
            start_deal(which, h)

    def held(which, back, slot):
        at = pl.ds(slot * rows, rows)
        return (kcat.at[back, at, pl.ds(0, width)], vbuf.at[back, :, at])[which]

    def dealt(which, slot):
        if which == QUERIES:
            block = qcat.at[mine, pl.ds(slot * rows, rows), pl.ds(0, width)]
        else:
            block = held(which, 0, slot)
        pltpu.make_async_copy(block, block, deal_recv.at[which, slot]).wait()

    def pass_on(which, back, slot):
        return pltpu.make_async_remote_copy(
            src_ref=held(which, 0, slot),
            dst_ref=held(which, back, slot),
            send_sem=pass_send.at[which, back - 1, slot],
            recv_sem=pass_recv.at[which, back - 1, slot],
            device_id={"blk": me + back * CELL},
            device_id_type=MESH,
        )

    def first_passes(which):
        for slot in range(SIDE):
            dealt(which, slot)
            for back in (1, 2):

                @pl.when(me + back * CELL < count)
                def _():
                    pass_on(which, back, slot).start()

    def passed(which):
        for back in (1, 2):

            @pl.when(cell >= back)
            def _():
                for slot in range(SIDE):
                    block = held(which, back, slot)
                    pltpu.make_async_copy(block, block, pass_recv.at[which, back - 1, slot]).wait()

    beside = mine + 1 - 2 * lax.rem(mine, 2)
    across = mine + 2 - 4 * (mine // 2)
    diagonal = SIDE - 1 - mine

    def share(group, to):
        block = qcat.at[group, :, pl.ds(0, width)]
        return pltpu.make_async_remote_copy(
            src_ref=block,
            dst_ref=block,
            send_sem=share_send.at[to],
            recv_sem=share_recv.at[group],
            device_id={"blk": quarter + to},
            device_id_type=MESH,
        )

    def shared(group):
        block = qcat.at[group, :, pl.ds(0, width)]
        pltpu.make_async_copy(block, block, share_recv.at[group]).wait()

    def share_own():
        for slot in range(SIDE):
            dealt(QUERIES, slot)
        share(mine, across).start()
        share(mine, beside).start()

    first_passes(KEYS)
    share_own()
    first_passes(VALUES)
    shared(across)
    hand_on = pltpu.make_async_remote_copy(
        src_ref=qcat.at[across, :, pl.ds(0, width)],
        dst_ref=qcat.at[across, :, pl.ds(0, width)],
        send_sem=share_send.at[diagonal],
        recv_sem=share_recv.at[across],
        device_id={"blk": quarter + beside},
        device_id_type=MESH,
    )
    hand_on.start()
    passed(KEYS)
    passed(VALUES)

    to_log2 = LOG2E / math.sqrt(width)

    def fold(combine, tile):
        return functools.reduce(combine, [tile[at : at + 8] for at in range(0, rows, 8)])

    def attend(first, pairs):
        group = mine if pairs == 3 else lax.rem(first + mine, SIDE)
        best = [jnp.full((8, rows), 2 * NEG, jnp.float32)] * SIDE
        for pair in range(pairs):
            m = first + pair * SIDE
            scores = lax.dot_general(
                kcat[(m + mine) // SIDE],
                qcat[group],
                (((1,), (1,)), ((), ())),
                preferred_element_type=jnp.float32,
            )
            for part in range(SIDE):
                for piece in range(SIDE):
                    shifted = (
                        scores[piece * rows : (piece + 1) * rows, part * rows : (part + 1) * rows]
                        * to_log2
                        + table[m * SIDE + part - piece + SIDE - 1]
                    )
                    shifts[pair, pl.ds(piece * rows, rows), pl.ds(part * rows, rows)] = shifted
                    best[part] = jnp.maximum(best[part], fold(jnp.maximum, shifted))
        tops = [jnp.max(tile, axis=0, keepdims=True) for tile in best]
        totals = [jnp.zeros((8, rows), jnp.float32)] * SIDE
        for pair in range(pairs):
            m = first + pair * SIDE
            probs = []
            for part in range(SIDE):
                weights = []
                for piece in range(SIDE):
                    shifted = shifts[pair, pl.ds(piece * rows, rows), pl.ds(part * rows, rows)]
                    weight = jnp.exp2(shifted - tops[part])
                    totals[part] = totals[part] + fold(jnp.add, weight)
                    weights.append(weight.astype(jnp.bfloat16))
                probs.append(jnp.concatenate(weights, axis=0))
            product = jnp.dot(
                vbuf[(m + mine) // SIDE],
                jnp.concatenate(probs, axis=1),
                preferred_element_type=jnp.float32,
            )
            acc[...] = product if pair == 0 else acc[...] + product
        for part in range(SIDE):
            total = jnp.sum(totals[part], axis=0, keepdims=True)
            level = tops[part] + jnp.log2(total)
            at = pl.ds(part * rows, rows)
            if pairs == 3:
                kept[:, at] = acc[:, at] / total
            else:
                part_out[group, :, at] = (acc[:, at] / total).astype(jnp.bfloat16)
            stat_out[group, pl.ds(part, 1), :] = level

    def hand_over(group):
        parts = [
            pltpu.make_async_remote_copy(
                src_ref=part_out.at[group, :, pl.ds(part * rows, rows)],
                dst_ref=part_in.at[mine, :, pl.ds(part * rows, rows)],
                send_sem=part_send.at[group, part],
                recv_sem=part_recv.at[mine, part],
                device_id={"blk": quarter + group},
                device_id_type=MESH,
            )
            for part in range(SIDE)
        ]
        stat = pltpu.make_async_remote_copy(
            src_ref=stat_out.at[group],
            dst_ref=stat_in.at[mine],
            send_sem=stat_send.at[group],
            recv_sem=stat_recv.at[mine],
            device_id={"blk": quarter + group},
            device_id_type=MESH,
        )
        return [stat] + parts

    def turn(group, _):
        @pl.when(group == mine)
        def _():
            attend(0, 3)

        @pl.when(group != mine)
        def _():
            @pl.when(group != across)
            def _():
                shared(group)

            attend(lax.rem(group - mine + SIDE, SIDE), 2)
            for copy in hand_over(group):
                copy.start()

        return 0

    lax.fori_loop(0, SIDE, turn, 0)

    others = [lax.rem(mine + step, SIDE) for step in range(1, SIDE)]
    for other in others:
        block = stat_in.at[other]
        pltpu.make_async_copy(block, block, stat_recv.at[other]).wait()

    def home(part):
        src = merged.at[pl.ds(part * rows, rows)]
        dst = out_ref.at[:, pl.ds(pl.multiple_of(head * width, width), width)]
        return src, dst, base + mine * SIDE + part

    def send_home(part):
        src, dst, target = home(part)
        return pltpu.make_async_remote_copy(
            src_ref=src,
            dst_ref=dst,
            send_sem=back_send.at[part],
            recv_sem=back_recv.at[head],
            device_id={"blk": target},
            device_id_type=MESH,
        )

    for part in range(SIDE):
        at = pl.ds(part * rows, rows)
        for other in others:
            block = part_in.at[other, :, at]
            pltpu.make_async_copy(block, block, part_recv.at[other, part]).wait()
        values = [kept[:, at]] + [part_in[other, :, at] for other in others]
        levels = [stat_out[mine, pl.ds(part, 1), :]]
        levels += [stat_in[other, pl.ds(part, 1), :] for other in others]
        most = functools.reduce(jnp.maximum, levels)
        shares = [jnp.exp2(level - most) for level in levels]
        total = functools.reduce(jnp.add, shares)
        whole = [v.astype(jnp.float32) * s for v, s in zip(values, shares)]
        whole = functools.reduce(jnp.add, whole) / total
        merged[at, :] = whole.T.astype(jnp.bfloat16)
        src, dst, target = home(part)

        @pl.when(target != me)
        def _():
            send_home(part).start()

        @pl.when(target == me)
        def _():
            pltpu.make_async_copy(src, dst, back_recv.at[head]).start()

    for h in range(SIDE):
        block = out_ref.at[:, pl.ds(h * width, width)]
        pltpu.make_async_copy(block, block, back_recv.at[h]).wait()

    for which in range(3):
        for h in range(SIDE):
            end_deal(which, h)
    share(mine, across).wait_send()
    share(mine, beside).wait_send()
    hand_on.wait_send()
    for which in (KEYS, VALUES):
        for back in (1, 2):

            @pl.when(me + back * CELL < count)
            def _():
                for slot in range(SIDE):
                    pass_on(which, back, slot).wait_send()

    for other in others:
        for copy in hand_over(other):
            copy.wait_send()
    for part in range(SIDE):

        @pl.when(base + mine * SIDE + part != me)
        def _():
            send_home(part).wait_send()


def on_device(query_rows, key_rows, value_rows, kerple_power, kerple_scale, doc_lengths):
    count = lax.axis_size("blk")
    rows, columns = query_rows.shape
    width = columns // SIDE
    span = SIDE * rows
    return pl.pallas_call(
        functools.partial(kernel, rows, width, count),
        out_shape=pltpu.VMEM((rows, columns), jnp.bfloat16),
        in_specs=[pl.BlockSpec(memory_space=pltpu.SMEM)] * 3 + [pl.BlockSpec(memory_space=pl.ANY)] * 3,
        out_specs=pl.BlockSpec(memory_space=pltpu.VMEM),
        scratch_shapes=[
            pltpu.VMEM((rows, columns), jnp.bfloat16),
            pltpu.VMEM((rows, columns), jnp.bfloat16),
            pltpu.VMEM((rows, columns), jnp.bfloat16),
            pltpu.VMEM((SIDE, width, rows), jnp.bfloat16),
            pltpu.VMEM((SIDE, span, 2 * width), jnp.bfloat16),
            pltpu.VMEM((3, span, 2 * width), jnp.bfloat16),
            pltpu.VMEM((3, width, span), jnp.bfloat16),
            pltpu.VMEM((3, span, span), jnp.float32),
            pltpu.VMEM((width, span), jnp.float32),
            pltpu.VMEM((2 * CELL + 2 * SIDE - 1, rows, rows), jnp.float32),
            pltpu.VMEM((SIDE, width, span), jnp.bfloat16),
            pltpu.VMEM((SIDE, 2 * SIDE, rows), jnp.float32),
            pltpu.VMEM((SIDE, width, span), jnp.bfloat16),
            pltpu.VMEM((SIDE, 2 * SIDE, rows), jnp.float32),
            pltpu.VMEM((width, span), jnp.float32),
            pltpu.VMEM((span, width), jnp.bfloat16),
            pltpu.SemaphoreType.DMA((3,)),
            pltpu.SemaphoreType.DMA((3, SIDE)),
            pltpu.SemaphoreType.DMA((3, SIDE)),
            pltpu.SemaphoreType.DMA((2, 2, SIDE)),
            pltpu.SemaphoreType.DMA((2, 2, SIDE)),
            pltpu.SemaphoreType.DMA((SIDE,)),
            pltpu.SemaphoreType.DMA((SIDE,)),
            pltpu.SemaphoreType.DMA((SIDE, SIDE)),
            pltpu.SemaphoreType.DMA((SIDE, SIDE)),
            pltpu.SemaphoreType.DMA((SIDE,)),
            pltpu.SemaphoreType.DMA((SIDE,)),
            pltpu.SemaphoreType.DMA((SIDE,)),
            pltpu.SemaphoreType.DMA((SIDE,)),
        ],
        compiler_params=pltpu.CompilerParams(
            collective_id=0, has_side_effects=True, vmem_limit_bytes=60 * 2**20
        ),
    )(kerple_power, kerple_scale, doc_lengths, query_rows, key_rows, value_rows)


def solution(mesh):
    block = P(("seq", "blk"), "head")
    return jax.shard_map(
        on_device,
        mesh=mesh,
        in_specs=(block, block, block, P("head"), P("head"), P("seq")),
        out_specs=block,
        check_vma=False,
    )
```

```python
import functools
import math

import jax
import jax.numpy as jnp
from jax import lax
from jax.experimental import pallas as pl
from jax.experimental.pallas import tpu as pltpu
from jax.sharding import PartitionSpec as P

MESH = pl.DeviceIdType.MESH
NEG = -1e30
TINY = 1e-30
SIDE = 4
CELL = SIDE * SIDE
LOG2E = math.log2(math.e)
KEYS, VALUES, QUERIES = 0, 1, 2
EARLY, LATE = (KEYS, QUERIES), (VALUES,)


def kernel(
    rows,
    width,
    count,
    power_ref,
    scale_ref,
    lengths_ref,
    q_ref,
    k_ref,
    v_ref,
    out_ref,
    k_here,
    q_here,
    straight,
    turned,
    qcat,
    kcat,
    vbuf,
    shifts,
    acc,
    table,
    part_out,
    stat_out,
    part_in,
    stat_in,
    kept,
    merged,
    fetch_sem,
    deal_send,
    deal_recv,
    pass_send,
    pass_recv,
    share_send,
    share_recv,
    part_send,
    part_recv,
    stat_send,
    stat_recv,
    back_send,
    back_recv,
):
    me = lax.axis_index("blk")
    cell = me // CELL
    base = cell * CELL
    place = me - base
    head = place // SIDE
    mine = place % SIDE
    quarter = base + head * SIDE
    span = SIDE * rows

    barrier = pltpu.get_barrier_semaphore()
    fetch = pltpu.make_async_copy(v_ref, straight, fetch_sem.at[0])
    near_k = pltpu.make_async_copy(k_ref, k_here, fetch_sem.at[1])
    near_q = pltpu.make_async_copy(q_ref, q_here, fetch_sem.at[2])
    near_k.start()
    near_q.start()
    fetch.start()
    peers = 0
    up, down = me + CELL, me - CELL
    for n in range(SIDE):
        dealt_to, dealt_by, near = base + n * SIDE + head, base + mine * SIDE + n, quarter + n
        for other, meet in (
            (dealt_to, dealt_to != me),
            (dealt_by, (dealt_by != me) & (n != head)),
            (near, (near != me) & (mine != head) & (n != head)),
        ):
            peers = peers + meet.astype(jnp.int32)

            @pl.when(meet)
            def _():
                pl.semaphore_signal(barrier, inc=1, device_id={"blk": other}, device_id_type=MESH)

    for other, meet in (
        (up, up < count),
        (down, down >= 0),
        (up + CELL, up + CELL < count),
        (down - CELL, down >= CELL),
    ):
        peers = peers + meet.astype(jnp.int32)

        @pl.when(meet)
        def _():
            pl.semaphore_signal(barrier, inc=1, device_id={"blk": other}, device_id_type=MESH)

    near_k.wait()
    near_q.wait()
    pl.semaphore_wait(barrier, peers)

    own = pl.ds(pl.multiple_of(mine * rows, rows), rows)

    def deal(which, h):
        columns = pl.ds(h * width, width)
        src = (k_here.at[:, columns], turned.at[h], q_here.at[:, columns])[which]
        dst = (
            kcat.at[0, own, pl.ds(0, width)],
            vbuf.at[0, :, own],
            qcat.at[head, own, pl.ds(0, width)],
        )[which]
        return src, dst

    def start_deal(which, h):
        target = base + h * SIDE + head
        src, dst = deal(which, h)

        @pl.when(target != me)
        def _():
            pltpu.make_async_remote_copy(
                src_ref=src,
                dst_ref=dst,
                send_sem=deal_send.at[which, h],
                recv_sem=deal_recv.at[which, mine],
                device_id={"blk": target},
                device_id_type=MESH,
            ).start()

        @pl.when(target == me)
        def _():
            pltpu.make_async_copy(src, dst, deal_recv.at[which, mine]).start()

    def end_deal(which, h):
        src, _ = deal(which, h)

        @pl.when(base + h * SIDE + head != me)
        def _():
            pltpu.make_async_copy(src, src, deal_send.at[which, h]).wait()

    def turn_values():
        fetch.wait()
        for h in range(SIDE):
            block = straight[:, h * width : (h + 1) * width].astype(jnp.float32)
            turned[h] = block.T.astype(jnp.bfloat16)

    for which in EARLY:
        if which == VALUES:
            turn_values()
        for h in range(SIDE):
            start_deal(which, h)

    row_at = lax.broadcasted_iota(jnp.int32, (rows, rows), 0)
    col_at = lax.broadcasted_iota(jnp.int32, (rows, rows), 1)
    power = power_ref[head] * (-LOG2E)
    scale = scale_ref[head]

    def fill_table(at, _):
        distance = (at - (SIDE - 1)) * rows + col_at - row_at
        far = jnp.maximum(distance, 0).astype(jnp.float32)
        table[at] = jnp.where(distance >= 0, power * jnp.log(1.0 + scale * far), NEG)
        return 0

    lax.fori_loop(0, table.shape[0], fill_table, 0)

    ends = []
    for doc in range(lengths_ref.shape[0]):
        ends.append(lengths_ref[doc] + (ends[-1] if ends else 0))
    lane = lax.broadcasted_iota(jnp.int32, (rows, width), 1)
    line = lax.broadcasted_iota(jnp.int32, (rows, width), 0)

    def in_doc(start):
        position = line + start
        doc = jnp.zeros((rows, width), jnp.int32)
        for end in ends:
            doc = doc + (position >= end).astype(jnp.int32)
        return (doc == lane) & (position >= 0)

    def fill_query(at, _):
        group, part = at // SIDE, at % SIDE
        same = in_doc(base * rows + at * rows)
        where_to = pl.ds(pl.multiple_of(part * rows, rows), rows)
        qcat[group, where_to, pl.ds(width, width)] = jnp.where(same, 1.0, 0.0).astype(jnp.bfloat16)
        return 0

    def fill_key(at, _):
        back, part = at // SIDE, at % SIDE
        same = in_doc((base - back * CELL + mine * SIDE + part) * rows)
        fill = jnp.where(same | (lane >= len(ends)), 0.0, NEG).astype(jnp.bfloat16)
        where_to = pl.ds(pl.multiple_of(part * rows, rows), rows)
        kcat[back, where_to, pl.ds(width, width)] = fill
        return 0

    lax.fori_loop(0, CELL, fill_query, 0)
    lax.fori_loop(0, 3 * SIDE, fill_key, 0)

    def blank(back, _):
        kcat[back, :, pl.ds(0, width)] = jnp.zeros((span, width), jnp.bfloat16)
        vbuf[back] = jnp.zeros((width, span), jnp.bfloat16)
        return 0

    lax.fori_loop(jnp.minimum(cell + 1, 3), 3, blank, 0)
    for which in LATE:
        if which == VALUES:
            turn_values()
        for h in range(SIDE):
            start_deal(which, h)

    def held(which, back, slot):
        at = pl.ds(slot * rows, rows)
        return (kcat.at[back, at, pl.ds(0, width)], vbuf.at[back, :, at])[which]

    def dealt(which, slot):
        if which == QUERIES:
            block = qcat.at[mine, pl.ds(slot * rows, rows), pl.ds(0, width)]
        else:
            block = held(which, 0, slot)
        pltpu.make_async_copy(block, block, deal_recv.at[which, slot]).wait()

    def pass_on(which, back, slot):
        return pltpu.make_async_remote_copy(
            src_ref=held(which, 0, slot),
            dst_ref=held(which, back, slot),
            send_sem=pass_send.at[which, back - 1, slot],
            recv_sem=pass_recv.at[which, back - 1, slot],
            device_id={"blk": me + back * CELL},
            device_id_type=MESH,
        )

    def first_passes(which):
        for slot in range(SIDE):
            dealt(which, slot)
            for back in (1, 2):

                @pl.when(me + back * CELL < count)
                def _():
                    pass_on(which, back, slot).start()

    def passed(back):
        @pl.when(cell >= back)
        def _():
            for which in (KEYS, VALUES):
                for slot in range(SIDE):
                    block = held(which, back, slot)
                    pltpu.make_async_copy(block, block, pass_recv.at[which, back - 1, slot]).wait()

    beside = mine + 1 - 2 * lax.rem(mine, 2)
    across = mine + 2 - 4 * (mine // 2)
    diagonal = SIDE - 1 - mine

    def share(group, to):
        block = qcat.at[group, :, pl.ds(0, width)]
        return pltpu.make_async_remote_copy(
            src_ref=block,
            dst_ref=block,
            send_sem=share_send.at[to],
            recv_sem=share_recv.at[group],
            device_id={"blk": quarter + to},
            device_id_type=MESH,
        )

    def shared(group):
        block = qcat.at[group, :, pl.ds(0, width)]
        pltpu.make_async_copy(block, block, share_recv.at[group]).wait()

    def share_own():
        for slot in range(SIDE):
            dealt(QUERIES, slot)
        share(mine, across).start()
        share(mine, beside).start()

    first_passes(KEYS)
    share_own()
    first_passes(VALUES)
    shared(across)
    hand_on = pltpu.make_async_remote_copy(
        src_ref=qcat.at[across, :, pl.ds(0, width)],
        dst_ref=qcat.at[across, :, pl.ds(0, width)],
        send_sem=share_send.at[diagonal],
        recv_sem=share_recv.at[across],
        device_id={"blk": quarter + beside},
        device_id_type=MESH,
    )
    hand_on.start()
    passed(1)

    to_log2 = LOG2E / math.sqrt(width)

    def fold(combine, tile):
        return functools.reduce(combine, [tile[at : at + 8] for at in range(0, rows, 8)])

    def attend(first, pairs):
        group = mine if pairs == 3 else lax.rem(first + mine, SIDE)
        best = [jnp.full((8, rows), 2 * NEG, jnp.float32)] * SIDE
        for pair in range(pairs):
            m = first + pair * SIDE
            scores = lax.dot_general(
                kcat[(m + mine) // SIDE],
                qcat[group],
                (((1,), (1,)), ((), ())),
                preferred_element_type=jnp.float32,
            )
            for part in range(SIDE):
                for piece in range(SIDE):
                    shifted = (
                        scores[piece * rows : (piece + 1) * rows, part * rows : (part + 1) * rows]
                        * to_log2
                        + table[m * SIDE + part - piece + SIDE - 1]
                    )
                    shifts[pair, pl.ds(piece * rows, rows), pl.ds(part * rows, rows)] = shifted
                    best[part] = jnp.maximum(best[part], fold(jnp.maximum, shifted))
        tops = [jnp.max(tile, axis=0, keepdims=True) for tile in best]
        totals = [jnp.zeros((8, rows), jnp.float32)] * SIDE
        for pair in range(pairs):
            m = first + pair * SIDE
            probs = []
            for part in range(SIDE):
                weights = []
                for piece in range(SIDE):
                    shifted = shifts[pair, pl.ds(piece * rows, rows), pl.ds(part * rows, rows)]
                    weight = jnp.exp2(shifted - tops[part])
                    totals[part] = totals[part] + fold(jnp.add, weight)
                    weights.append(weight.astype(jnp.bfloat16))
                probs.append(jnp.concatenate(weights, axis=0))
            product = jnp.dot(
                vbuf[(m + mine) // SIDE],
                jnp.concatenate(probs, axis=1),
                preferred_element_type=jnp.float32,
            )
            acc[...] = product if pair == 0 else acc[...] + product
        for part in range(SIDE):
            total = jnp.sum(totals[part], axis=0, keepdims=True)
            level = tops[part] + jnp.log2(total)
            at = pl.ds(part * rows, rows)
            if pairs == 3:
                kept[:, at] = acc[:, at] / total
            else:
                part_out[group, :, at] = (acc[:, at] / total).astype(jnp.bfloat16)
            stat_out[group, pl.ds(part, 1), :] = level

    def hand_over(group):
        parts = [
            pltpu.make_async_remote_copy(
                src_ref=part_out.at[group, :, pl.ds(part * rows, rows)],
                dst_ref=part_in.at[mine, :, pl.ds(part * rows, rows)],
                send_sem=part_send.at[group, part],
                recv_sem=part_recv.at[mine, part],
                device_id={"blk": quarter + group},
                device_id_type=MESH,
            )
            for part in range(SIDE)
        ]
        stat = pltpu.make_async_remote_copy(
            src_ref=stat_out.at[group],
            dst_ref=stat_in.at[mine],
            send_sem=stat_send.at[group],
            recv_sem=stat_recv.at[mine],
            device_id={"blk": quarter + group},
            device_id_type=MESH,
        )
        return [stat] + parts

    def turn(order, _):
        group = order + (order >= mine).astype(jnp.int32)

        @pl.when(group != across)
        def _():
            shared(group)

        attend(lax.rem(group - mine + SIDE, SIDE), 2)
        for copy in hand_over(group):
            copy.start()
        return 0

    @pl.when(mine > 0)
    def _():
        passed(2)

    lax.fori_loop(0, SIDE - 1, turn, 0)

    @pl.when(mine == 0)
    def _():
        passed(2)

    attend(0, 3)

    others = [lax.rem(mine + step, SIDE) for step in range(1, SIDE)]
    for other in others:
        block = stat_in.at[other]
        pltpu.make_async_copy(block, block, stat_recv.at[other]).wait()

    def home(part):
        src = merged.at[pl.ds(part * rows, rows)]
        dst = out_ref.at[:, pl.ds(pl.multiple_of(head * width, width), width)]
        return src, dst, base + mine * SIDE + part

    def send_home(part):
        src, dst, target = home(part)
        return pltpu.make_async_remote_copy(
            src_ref=src,
            dst_ref=dst,
            send_sem=back_send.at[part],
            recv_sem=back_recv.at[head],
            device_id={"blk": target},
            device_id_type=MESH,
        )

    for part in range(SIDE):
        at = pl.ds(part * rows, rows)
        for other in others:
            block = part_in.at[other, :, at]
            pltpu.make_async_copy(block, block, part_recv.at[other, part]).wait()
        values = [kept[:, at]] + [part_in[other, :, at] for other in others]
        levels = [stat_out[mine, pl.ds(part, 1), :]]
        levels += [stat_in[other, pl.ds(part, 1), :] for other in others]
        most = functools.reduce(jnp.maximum, levels)
        shares = [jnp.exp2(level - most) for level in levels]
        total = functools.reduce(jnp.add, shares)
        whole = [v.astype(jnp.float32) * s for v, s in zip(values, shares)]
        whole = functools.reduce(jnp.add, whole) / total
        merged[at, :] = whole.T.astype(jnp.bfloat16)
        src, dst, target = home(part)

        @pl.when(target != me)
        def _():
            send_home(part).start()

        @pl.when(target == me)
        def _():
            pltpu.make_async_copy(src, dst, back_recv.at[head]).start()

    for h in range(SIDE):
        block = out_ref.at[:, pl.ds(h * width, width)]
        pltpu.make_async_copy(block, block, back_recv.at[h]).wait()

    for which in range(3):
        for h in range(SIDE):
            end_deal(which, h)
    share(mine, across).wait_send()
    share(mine, beside).wait_send()
    hand_on.wait_send()
    for which in (KEYS, VALUES):
        for back in (1, 2):

            @pl.when(me + back * CELL < count)
            def _():
                for slot in range(SIDE):
                    pass_on(which, back, slot).wait_send()

    for other in others:
        for copy in hand_over(other):
            copy.wait_send()
    for part in range(SIDE):

        @pl.when(base + mine * SIDE + part != me)
        def _():
            send_home(part).wait_send()


def on_device(query_rows, key_rows, value_rows, kerple_power, kerple_scale, doc_lengths):
    count = lax.axis_size("blk")
    rows, columns = query_rows.shape
    width = columns // SIDE
    span = SIDE * rows
    return pl.pallas_call(
        functools.partial(kernel, rows, width, count),
        out_shape=pltpu.VMEM((rows, columns), jnp.bfloat16),
        in_specs=[pl.BlockSpec(memory_space=pltpu.SMEM)] * 3 + [pl.BlockSpec(memory_space=pl.ANY)] * 3,
        out_specs=pl.BlockSpec(memory_space=pltpu.VMEM),
        scratch_shapes=[
            pltpu.VMEM((rows, columns), jnp.bfloat16),
            pltpu.VMEM((rows, columns), jnp.bfloat16),
            pltpu.VMEM((rows, columns), jnp.bfloat16),
            pltpu.VMEM((SIDE, width, rows), jnp.bfloat16),
            pltpu.VMEM((SIDE, span, 2 * width), jnp.bfloat16),
            pltpu.VMEM((3, span, 2 * width), jnp.bfloat16),
            pltpu.VMEM((3, width, span), jnp.bfloat16),
            pltpu.VMEM((3, span, span), jnp.float32),
            pltpu.VMEM((width, span), jnp.float32),
            pltpu.VMEM((2 * CELL + 2 * SIDE - 1, rows, rows), jnp.float32),
            pltpu.VMEM((SIDE, width, span), jnp.bfloat16),
            pltpu.VMEM((SIDE, 2 * SIDE, rows), jnp.float32),
            pltpu.VMEM((SIDE, width, span), jnp.bfloat16),
            pltpu.VMEM((SIDE, 2 * SIDE, rows), jnp.float32),
            pltpu.VMEM((width, span), jnp.float32),
            pltpu.VMEM((span, width), jnp.bfloat16),
            pltpu.SemaphoreType.DMA((3,)),
            pltpu.SemaphoreType.DMA((3, SIDE)),
            pltpu.SemaphoreType.DMA((3, SIDE)),
            pltpu.SemaphoreType.DMA((2, 2, SIDE)),
            pltpu.SemaphoreType.DMA((2, 2, SIDE)),
            pltpu.SemaphoreType.DMA((SIDE,)),
            pltpu.SemaphoreType.DMA((SIDE,)),
            pltpu.SemaphoreType.DMA((SIDE, SIDE)),
            pltpu.SemaphoreType.DMA((SIDE, SIDE)),
            pltpu.SemaphoreType.DMA((SIDE,)),
            pltpu.SemaphoreType.DMA((SIDE,)),
            pltpu.SemaphoreType.DMA((SIDE,)),
            pltpu.SemaphoreType.DMA((SIDE,)),
        ],
        compiler_params=pltpu.CompilerParams(
            collective_id=0, has_side_effects=True, vmem_limit_bytes=60 * 2**20
        ),
    )(kerple_power, kerple_scale, doc_lengths, query_rows, key_rows, value_rows)


def solution(mesh):
    block = P(("seq", "blk"), "head")
    return jax.shard_map(
        on_device,
        mesh=mesh,
        in_specs=(block, block, block, P("head"), P("head"), P("seq")),
        out_specs=block,
        check_vma=False,
    )
```

```python
import functools
import math

import jax
import jax.numpy as jnp
from jax import lax
from jax.experimental import pallas as pl
from jax.experimental.pallas import tpu as pltpu
from jax.sharding import PartitionSpec as P

MESH = pl.DeviceIdType.MESH
NEG = -1e30
TINY = 1e-30
SIDE = 4
CELL = SIDE * SIDE
LOG2E = math.log2(math.e)
KEYS, VALUES, QUERIES = 0, 1, 2
EARLY, LATE = (KEYS, QUERIES), (VALUES,)


def kernel(
    rows,
    width,
    count,
    power_ref,
    scale_ref,
    lengths_ref,
    q_ref,
    k_ref,
    v_ref,
    out_ref,
    k_here,
    q_here,
    straight,
    turned,
    qcat,
    kcat,
    vbuf,
    shifts,
    acc,
    table,
    part_out,
    stat_out,
    part_in,
    stat_in,
    kept,
    merged,
    fetch_sem,
    deal_send,
    deal_recv,
    pass_send,
    pass_recv,
    share_send,
    share_recv,
    part_send,
    part_recv,
    stat_send,
    stat_recv,
    back_send,
    back_recv,
):
    me = lax.axis_index("blk")
    cell = me // CELL
    base = cell * CELL
    place = me - base
    head = place // SIDE
    mine = place % SIDE
    quarter = base + head * SIDE
    span = SIDE * rows

    barrier = pltpu.get_barrier_semaphore()
    fetch = pltpu.make_async_copy(v_ref, straight, fetch_sem.at[0])
    near_k = pltpu.make_async_copy(k_ref, k_here, fetch_sem.at[1])
    near_q = pltpu.make_async_copy(q_ref, q_here, fetch_sem.at[2])
    near_k.start()
    near_q.start()
    fetch.start()
    peers = 0
    up, down = me + CELL, me - CELL
    for n in range(SIDE):
        dealt_to, dealt_by, near = base + n * SIDE + head, base + mine * SIDE + n, quarter + n
        for other, meet in (
            (dealt_to, dealt_to != me),
            (dealt_by, (dealt_by != me) & (n != head)),
            (near, (near != me) & (mine != head) & (n != head)),
        ):
            peers = peers + meet.astype(jnp.int32)

            @pl.when(meet)
            def _():
                pl.semaphore_signal(barrier, inc=1, device_id={"blk": other}, device_id_type=MESH)

    for other, meet in (
        (up, up < count),
        (down, down >= 0),
        (up + CELL, up + CELL < count),
        (down - CELL, down >= CELL),
    ):
        peers = peers + meet.astype(jnp.int32)

        @pl.when(meet)
        def _():
            pl.semaphore_signal(barrier, inc=1, device_id={"blk": other}, device_id_type=MESH)

    near_k.wait()
    near_q.wait()
    pl.semaphore_wait(barrier, peers)

    own = pl.ds(pl.multiple_of(mine * rows, rows), rows)

    def deal(which, h):
        columns = pl.ds(h * width, width)
        src = (k_here.at[:, columns], turned.at[h], q_here.at[:, columns])[which]
        dst = (
            kcat.at[0, own, pl.ds(0, width)],
            vbuf.at[0, :, own],
            qcat.at[head, own, pl.ds(0, width)],
        )[which]
        return src, dst

    def start_deal(which, h):
        target = base + h * SIDE + head
        src, dst = deal(which, h)

        @pl.when(target != me)
        def _():
            pltpu.make_async_remote_copy(
                src_ref=src,
                dst_ref=dst,
                send_sem=deal_send.at[which, h],
                recv_sem=deal_recv.at[which, mine],
                device_id={"blk": target},
                device_id_type=MESH,
            ).start()

        @pl.when(target == me)
        def _():
            pltpu.make_async_copy(src, dst, deal_recv.at[which, mine]).start()

    def end_deal(which, h):
        src, _ = deal(which, h)

        @pl.when(base + h * SIDE + head != me)
        def _():
            pltpu.make_async_copy(src, src, deal_send.at[which, h]).wait()

    def turn_values():
        fetch.wait()
        for h in range(SIDE):
            block = straight[:, h * width : (h + 1) * width].astype(jnp.float32)
            turned[h] = block.T.astype(jnp.bfloat16)

    for which in EARLY:
        if which == VALUES:
            turn_values()
        for h in range(SIDE):
            start_deal(which, h)

    row_at = lax.broadcasted_iota(jnp.int32, (rows, rows), 0)
    col_at = lax.broadcasted_iota(jnp.int32, (rows, rows), 1)
    power = power_ref[head] * (-LOG2E)
    scale = scale_ref[head]

    def fill_table(at, _):
        distance = (at - (SIDE - 1)) * rows + col_at - row_at
        far = jnp.maximum(distance, 0).astype(jnp.float32)
        table[at] = jnp.where(distance >= 0, power * jnp.log(1.0 + scale * far), NEG)
        return 0

    lax.fori_loop(0, table.shape[0], fill_table, 0)

    ends = []
    for doc in range(lengths_ref.shape[0]):
        ends.append(lengths_ref[doc] + (ends[-1] if ends else 0))
    lane = lax.broadcasted_iota(jnp.int32, (rows, width), 1)
    line = lax.broadcasted_iota(jnp.int32, (rows, width), 0)

    def in_doc(start):
        position = line + start
        doc = jnp.zeros((rows, width), jnp.int32)
        for end in ends:
            doc = doc + (position >= end).astype(jnp.int32)
        return (doc == lane) & (position >= 0)

    def fill_query(at, _):
        group, part = at // SIDE, at % SIDE
        same = in_doc(base * rows + at * rows)
        where_to = pl.ds(pl.multiple_of(part * rows, rows), rows)
        qcat[group, where_to, pl.ds(width, width)] = jnp.where(same, 1.0, 0.0).astype(jnp.bfloat16)
        return 0

    def fill_key(at, _):
        back, part = at // SIDE, at % SIDE
        same = in_doc((base - back * CELL + mine * SIDE + part) * rows)
        fill = jnp.where(same | (lane >= len(ends)), 0.0, NEG).astype(jnp.bfloat16)
        where_to = pl.ds(pl.multiple_of(part * rows, rows), rows)
        kcat[back, where_to, pl.ds(width, width)] = fill
        return 0

    lax.fori_loop(0, CELL, fill_query, 0)
    lax.fori_loop(0, 3 * SIDE, fill_key, 0)

    def blank(back, _):
        kcat[back, :, pl.ds(0, width)] = jnp.zeros((span, width), jnp.bfloat16)
        vbuf[back] = jnp.zeros((width, span), jnp.bfloat16)
        return 0

    lax.fori_loop(jnp.minimum(cell + 1, 3), 3, blank, 0)
    for which in LATE:
        if which == VALUES:
            turn_values()
        for h in range(SIDE):
            start_deal(which, h)

    def held(which, back, slot):
        at = pl.ds(slot * rows, rows)
        return (kcat.at[back, at, pl.ds(0, width)], vbuf.at[back, :, at])[which]

    def dealt(which, slot):
        if which == QUERIES:
            block = qcat.at[mine, pl.ds(slot * rows, rows), pl.ds(0, width)]
        else:
            block = held(which, 0, slot)
        pltpu.make_async_copy(block, block, deal_recv.at[which, slot]).wait()

    def pass_on(which, back, slot):
        return pltpu.make_async_remote_copy(
            src_ref=held(which, 0, slot),
            dst_ref=held(which, back, slot),
            send_sem=pass_send.at[which, back - 1, slot],
            recv_sem=pass_recv.at[which, back - 1, slot],
            device_id={"blk": me + back * CELL},
            device_id_type=MESH,
        )

    def first_passes(which):
        for slot in range(SIDE):
            dealt(which, slot)
            for back in (1, 2):

                @pl.when(me + back * CELL < count)
                def _():
                    pass_on(which, back, slot).start()

    def passed(which, back, needed):
        @pl.when((cell >= back) & needed)
        def _():
            for slot in range(SIDE):
                block = held(which, back, slot)
                pltpu.make_async_copy(block, block, pass_recv.at[which, back - 1, slot]).wait()

    beside = mine + 1 - 2 * lax.rem(mine, 2)
    across = mine + 2 - 4 * (mine // 2)
    diagonal = SIDE - 1 - mine

    def share(group, to):
        block = qcat.at[group, :, pl.ds(0, width)]
        return pltpu.make_async_remote_copy(
            src_ref=block,
            dst_ref=block,
            send_sem=share_send.at[to],
            recv_sem=share_recv.at[group],
            device_id={"blk": quarter + to},
            device_id_type=MESH,
        )

    def shared(group):
        block = qcat.at[group, :, pl.ds(0, width)]
        pltpu.make_async_copy(block, block, share_recv.at[group]).wait()

    def share_own():
        for slot in range(SIDE):
            dealt(QUERIES, slot)
        share(mine, across).start()
        share(mine, beside).start()

    first_passes(KEYS)
    share_own()
    first_passes(VALUES)
    shared(across)
    hand_on = pltpu.make_async_remote_copy(
        src_ref=qcat.at[across, :, pl.ds(0, width)],
        dst_ref=qcat.at[across, :, pl.ds(0, width)],
        send_sem=share_send.at[diagonal],
        recv_sem=share_recv.at[across],
        device_id={"blk": quarter + beside},
        device_id_type=MESH,
    )
    hand_on.start()
    passed(KEYS, 1, True)
    passed(KEYS, 2, mine > 0)

    to_log2 = LOG2E / math.sqrt(width)

    def fold(combine, tile):
        return functools.reduce(combine, [tile[at : at + 8] for at in range(0, rows, 8)])

    def attend(first, pairs, await_values):
        group = mine if pairs == 3 else lax.rem(first + mine, SIDE)
        best = [jnp.full((8, rows), 2 * NEG, jnp.float32)] * SIDE
        for pair in range(pairs):
            m = first + pair * SIDE
            scores = lax.dot_general(
                kcat[(m + mine) // SIDE],
                qcat[group],
                (((1,), (1,)), ((), ())),
                preferred_element_type=jnp.float32,
            )
            for part in range(SIDE):
                for piece in range(SIDE):
                    shifted = (
                        scores[piece * rows : (piece + 1) * rows, part * rows : (part + 1) * rows]
                        * to_log2
                        + table[m * SIDE + part - piece + SIDE - 1]
                    )
                    shifts[pair, pl.ds(piece * rows, rows), pl.ds(part * rows, rows)] = shifted
                    best[part] = jnp.maximum(best[part], fold(jnp.maximum, shifted))
        tops = [jnp.max(tile, axis=0, keepdims=True) for tile in best]
        await_values()
        totals = [jnp.zeros((8, rows), jnp.float32)] * SIDE
        for pair in range(pairs):
            m = first + pair * SIDE
            probs = []
            for part in range(SIDE):
                weights = []
                for piece in range(SIDE):
                    shifted = shifts[pair, pl.ds(piece * rows, rows), pl.ds(part * rows, rows)]
                    weight = jnp.exp2(shifted - tops[part])
                    totals[part] = totals[part] + fold(jnp.add, weight)
                    weights.append(weight.astype(jnp.bfloat16))
                probs.append(jnp.concatenate(weights, axis=0))
            product = jnp.dot(
                vbuf[(m + mine) // SIDE],
                jnp.concatenate(probs, axis=1),
                preferred_element_type=jnp.float32,
            )
            acc[...] = product if pair == 0 else acc[...] + product
        for part in range(SIDE):
            total = jnp.sum(totals[part], axis=0, keepdims=True)
            level = tops[part] + jnp.log2(total)
            at = pl.ds(part * rows, rows)
            if pairs == 3:
                kept[:, at] = acc[:, at] / total
            else:
                part_out[group, :, at] = (acc[:, at] / total).astype(jnp.bfloat16)
            stat_out[group, pl.ds(part, 1), :] = level

    def hand_over(group):
        parts = [
            pltpu.make_async_remote_copy(
                src_ref=part_out.at[group, :, pl.ds(part * rows, rows)],
                dst_ref=part_in.at[mine, :, pl.ds(part * rows, rows)],
                send_sem=part_send.at[group, part],
                recv_sem=part_recv.at[mine, part],
                device_id={"blk": quarter + group},
                device_id_type=MESH,
            )
            for part in range(SIDE)
        ]
        stat = pltpu.make_async_remote_copy(
            src_ref=stat_out.at[group],
            dst_ref=stat_in.at[mine],
            send_sem=stat_send.at[group],
            recv_sem=stat_recv.at[mine],
            device_id={"blk": quarter + group},
            device_id_type=MESH,
        )
        return [stat] + parts

    def turn(order, _):
        group = order + (order >= mine).astype(jnp.int32)

        @pl.when(group != across)
        def _():
            shared(group)

        def await_values():
            passed(VALUES, 1, order == 0)
            passed(VALUES, 2, (order == 0) & (mine > 0))

        attend(lax.rem(group - mine + SIDE, SIDE), 2, await_values)
        for copy in hand_over(group):
            copy.start()
        return 0

    lax.fori_loop(0, SIDE - 1, turn, 0)

    passed(KEYS, 2, mine == 0)
    attend(0, 3, lambda: passed(VALUES, 2, mine == 0))

    others = [lax.rem(mine + step, SIDE) for step in range(1, SIDE)]
    for other in others:
        block = stat_in.at[other]
        pltpu.make_async_copy(block, block, stat_recv.at[other]).wait()

    def home(part):
        src = merged.at[pl.ds(part * rows, rows)]
        dst = out_ref.at[:, pl.ds(pl.multiple_of(head * width, width), width)]
        return src, dst, base + mine * SIDE + part

    def send_home(part):
        src, dst, target = home(part)
        return pltpu.make_async_remote_copy(
            src_ref=src,
            dst_ref=dst,
            send_sem=back_send.at[part],
            recv_sem=back_recv.at[head],
            device_id={"blk": target},
            device_id_type=MESH,
        )

    for part in range(SIDE):
        at = pl.ds(part * rows, rows)
        for other in others:
            block = part_in.at[other, :, at]
            pltpu.make_async_copy(block, block, part_recv.at[other, part]).wait()
        values = [kept[:, at]] + [part_in[other, :, at] for other in others]
        levels = [stat_out[mine, pl.ds(part, 1), :]]
        levels += [stat_in[other, pl.ds(part, 1), :] for other in others]
        most = functools.reduce(jnp.maximum, levels)
        shares = [jnp.exp2(level - most) for level in levels]
        total = functools.reduce(jnp.add, shares)
        whole = [v.astype(jnp.float32) * s for v, s in zip(values, shares)]
        whole = functools.reduce(jnp.add, whole) / total
        merged[at, :] = whole.T.astype(jnp.bfloat16)
        src, dst, target = home(part)

        @pl.when(target != me)
        def _():
            send_home(part).start()

        @pl.when(target == me)
        def _():
            pltpu.make_async_copy(src, dst, back_recv.at[head]).start()

    for h in range(SIDE):
        block = out_ref.at[:, pl.ds(h * width, width)]
        pltpu.make_async_copy(block, block, back_recv.at[h]).wait()

    for which in range(3):
        for h in range(SIDE):
            end_deal(which, h)
    share(mine, across).wait_send()
    share(mine, beside).wait_send()
    hand_on.wait_send()
    for which in (KEYS, VALUES):
        for back in (1, 2):

            @pl.when(me + back * CELL < count)
            def _():
                for slot in range(SIDE):
                    pass_on(which, back, slot).wait_send()

    for other in others:
        for copy in hand_over(other):
            copy.wait_send()
    for part in range(SIDE):

        @pl.when(base + mine * SIDE + part != me)
        def _():
            send_home(part).wait_send()


def on_device(query_rows, key_rows, value_rows, kerple_power, kerple_scale, doc_lengths):
    count = lax.axis_size("blk")
    rows, columns = query_rows.shape
    width = columns // SIDE
    span = SIDE * rows
    return pl.pallas_call(
        functools.partial(kernel, rows, width, count),
        out_shape=pltpu.VMEM((rows, columns), jnp.bfloat16),
        in_specs=[pl.BlockSpec(memory_space=pltpu.SMEM)] * 3 + [pl.BlockSpec(memory_space=pl.ANY)] * 3,
        out_specs=pl.BlockSpec(memory_space=pltpu.VMEM),
        scratch_shapes=[
            pltpu.VMEM((rows, columns), jnp.bfloat16),
            pltpu.VMEM((rows, columns), jnp.bfloat16),
            pltpu.VMEM((rows, columns), jnp.bfloat16),
            pltpu.VMEM((SIDE, width, rows), jnp.bfloat16),
            pltpu.VMEM((SIDE, span, 2 * width), jnp.bfloat16),
            pltpu.VMEM((3, span, 2 * width), jnp.bfloat16),
            pltpu.VMEM((3, width, span), jnp.bfloat16),
            pltpu.VMEM((3, span, span), jnp.float32),
            pltpu.VMEM((width, span), jnp.float32),
            pltpu.VMEM((2 * CELL + 2 * SIDE - 1, rows, rows), jnp.float32),
            pltpu.VMEM((SIDE, width, span), jnp.bfloat16),
            pltpu.VMEM((SIDE, 2 * SIDE, rows), jnp.float32),
            pltpu.VMEM((SIDE, width, span), jnp.bfloat16),
            pltpu.VMEM((SIDE, 2 * SIDE, rows), jnp.float32),
            pltpu.VMEM((width, span), jnp.float32),
            pltpu.VMEM((span, width), jnp.bfloat16),
            pltpu.SemaphoreType.DMA((3,)),
            pltpu.SemaphoreType.DMA((3, SIDE)),
            pltpu.SemaphoreType.DMA((3, SIDE)),
            pltpu.SemaphoreType.DMA((2, 2, SIDE)),
            pltpu.SemaphoreType.DMA((2, 2, SIDE)),
            pltpu.SemaphoreType.DMA((SIDE,)),
            pltpu.SemaphoreType.DMA((SIDE,)),
            pltpu.SemaphoreType.DMA((SIDE, SIDE)),
            pltpu.SemaphoreType.DMA((SIDE, SIDE)),
            pltpu.SemaphoreType.DMA((SIDE,)),
            pltpu.SemaphoreType.DMA((SIDE,)),
            pltpu.SemaphoreType.DMA((SIDE,)),
            pltpu.SemaphoreType.DMA((SIDE,)),
        ],
        compiler_params=pltpu.CompilerParams(
            collective_id=0, has_side_effects=True, vmem_limit_bytes=60 * 2**20
        ),
    )(kerple_power, kerple_scale, doc_lengths, query_rows, key_rows, value_rows)


def solution(mesh):
    block = P(("seq", "blk"), "head")
    return jax.shard_map(
        on_device,
        mesh=mesh,
        in_specs=(block, block, block, P("head"), P("head"), P("seq")),
        out_specs=block,
        check_vma=False,
    )
```

```python
import functools
import math

import jax
import jax.numpy as jnp
from jax import lax
from jax.experimental import pallas as pl
from jax.experimental.pallas import tpu as pltpu
from jax.sharding import PartitionSpec as P

MESH = pl.DeviceIdType.MESH
NEG = -1e30
TINY = 1e-30
SIDE = 4
CELL = SIDE * SIDE
LOG2E = math.log2(math.e)
KEYS, VALUES, QUERIES = 0, 1, 2
EARLY, LATE = (KEYS, QUERIES), (VALUES,)


def kernel(
    rows,
    width,
    count,
    power_ref,
    scale_ref,
    lengths_ref,
    q_ref,
    k_ref,
    v_ref,
    out_ref,
    k_here,
    q_here,
    straight,
    turned,
    qcat,
    kcat,
    vbuf,
    shifts,
    acc,
    table,
    part_out,
    stat_out,
    part_in,
    stat_in,
    kept,
    merged,
    fetch_sem,
    deal_send,
    deal_recv,
    pass_send,
    pass_recv,
    share_send,
    share_recv,
    part_send,
    part_recv,
    stat_send,
    stat_recv,
    back_send,
    back_recv,
):
    me = lax.axis_index("blk")
    cell = me // CELL
    base = cell * CELL
    place = me - base
    head = place // SIDE
    mine = place % SIDE
    quarter = base + head * SIDE
    span = SIDE * rows

    barrier = pltpu.get_barrier_semaphore()
    fetch = pltpu.make_async_copy(v_ref, straight, fetch_sem.at[0])
    near_k = pltpu.make_async_copy(k_ref, k_here, fetch_sem.at[1])
    near_q = pltpu.make_async_copy(q_ref, q_here, fetch_sem.at[2])
    near_k.start()
    near_q.start()
    fetch.start()
    peers = 0
    up, down = me + CELL, me - CELL
    for n in range(SIDE):
        dealt_to, dealt_by, near = base + n * SIDE + head, base + mine * SIDE + n, quarter + n
        for other, meet in (
            (dealt_to, dealt_to != me),
            (dealt_by, (dealt_by != me) & (n != head)),
            (near, (near != me) & (mine != head) & (n != head)),
        ):
            peers = peers + meet.astype(jnp.int32)

            @pl.when(meet)
            def _():
                pl.semaphore_signal(barrier, inc=1, device_id={"blk": other}, device_id_type=MESH)

    for other, meet in (
        (up, up < count),
        (down, down >= 0),
        (up + CELL, up + CELL < count),
        (down - CELL, down >= CELL),
    ):
        peers = peers + meet.astype(jnp.int32)

        @pl.when(meet)
        def _():
            pl.semaphore_signal(barrier, inc=1, device_id={"blk": other}, device_id_type=MESH)

    near_k.wait()
    near_q.wait()
    pl.semaphore_wait(barrier, peers)

    own = pl.ds(pl.multiple_of(mine * rows, rows), rows)

    def deal(which, h):
        columns = pl.ds(h * width, width)
        src = (k_here.at[:, columns], turned.at[h], q_here.at[:, columns])[which]
        dst = (
            kcat.at[0, own, pl.ds(0, width)],
            vbuf.at[0, :, own],
            qcat.at[head, own, pl.ds(0, width)],
        )[which]
        return src, dst

    def start_deal(which, h):
        target = base + h * SIDE + head
        src, dst = deal(which, h)

        @pl.when(target != me)
        def _():
            pltpu.make_async_remote_copy(
                src_ref=src,
                dst_ref=dst,
                send_sem=deal_send.at[which, h],
                recv_sem=deal_recv.at[which, mine],
                device_id={"blk": target},
                device_id_type=MESH,
            ).start()

        @pl.when(target == me)
        def _():
            pltpu.make_async_copy(src, dst, deal_recv.at[which, mine]).start()

    def end_deal(which, h):
        src, _ = deal(which, h)

        @pl.when(base + h * SIDE + head != me)
        def _():
            pltpu.make_async_copy(src, src, deal_send.at[which, h]).wait()

    def turn_values():
        fetch.wait()
        for h in range(SIDE):
            block = straight[:, h * width : (h + 1) * width].astype(jnp.float32)
            turned[h] = block.T.astype(jnp.bfloat16)

    for which in EARLY:
        if which == VALUES:
            turn_values()
        for h in range(SIDE):
            start_deal(which, h)

    row_at = lax.broadcasted_iota(jnp.int32, (rows, rows), 0)
    col_at = lax.broadcasted_iota(jnp.int32, (rows, rows), 1)
    power = power_ref[head] * (-LOG2E)
    scale = scale_ref[head]

    def fill_table(at, _):
        distance = (at - (SIDE - 1)) * rows + col_at - row_at
        far = jnp.maximum(distance, 0).astype(jnp.float32)
        table[at] = jnp.where(distance >= 0, power * jnp.log(1.0 + scale * far), NEG)
        return 0

    lax.fori_loop(0, table.shape[0], fill_table, 0)

    ends = []
    for doc in range(lengths_ref.shape[0]):
        ends.append(lengths_ref[doc] + (ends[-1] if ends else 0))
    lane = lax.broadcasted_iota(jnp.int32, (rows, width), 1)
    line = lax.broadcasted_iota(jnp.int32, (rows, width), 0)

    def in_doc(start):
        position = line + start
        doc = jnp.zeros((rows, width), jnp.int32)
        for end in ends:
            doc = doc + (position >= end).astype(jnp.int32)
        return (doc == lane) & (position >= 0)

    def fill_query(at, _):
        group, part = at // SIDE, at % SIDE
        same = in_doc(base * rows + at * rows)
        where_to = pl.ds(pl.multiple_of(part * rows, rows), rows)
        qcat[group, where_to, pl.ds(width, width)] = jnp.where(same, 1.0, 0.0).astype(jnp.bfloat16)
        return 0

    def fill_key(at, _):
        back, part = at // SIDE, at % SIDE
        same = in_doc((base - back * CELL + mine * SIDE + part) * rows)
        fill = jnp.where(same | (lane >= len(ends)), 0.0, NEG).astype(jnp.bfloat16)
        where_to = pl.ds(pl.multiple_of(part * rows, rows), rows)
        kcat[back, where_to, pl.ds(width, width)] = fill
        return 0

    lax.fori_loop(0, CELL, fill_query, 0)
    lax.fori_loop(0, 3 * SIDE, fill_key, 0)

    def blank(back, _):
        kcat[back, :, pl.ds(0, width)] = jnp.zeros((span, width), jnp.bfloat16)
        vbuf[back] = jnp.zeros((width, span), jnp.bfloat16)
        return 0

    lax.fori_loop(jnp.minimum(cell + 1, 3), 3, blank, 0)
    for which in LATE:
        if which == VALUES:
            turn_values()
        for h in range(SIDE):
            start_deal(which, h)

    def held(which, back, slot):
        at = pl.ds(slot * rows, rows)
        return (kcat.at[back, at, pl.ds(0, width)], vbuf.at[back, :, at])[which]

    def dealt(which, slot):
        if which == QUERIES:
            block = qcat.at[mine, pl.ds(slot * rows, rows), pl.ds(0, width)]
        else:
            block = held(which, 0, slot)
        pltpu.make_async_copy(block, block, deal_recv.at[which, slot]).wait()

    def pass_on(which, back, slot):
        return pltpu.make_async_remote_copy(
            src_ref=held(which, 0, slot),
            dst_ref=held(which, back, slot),
            send_sem=pass_send.at[which, back - 1, slot],
            recv_sem=pass_recv.at[which, back - 1, slot],
            device_id={"blk": me + back * CELL},
            device_id_type=MESH,
        )

    def first_passes(which):
        for slot in range(SIDE):
            dealt(which, slot)
            for back in (1, 2):

                @pl.when(me + back * CELL < count)
                def _():
                    pass_on(which, back, slot).start()

    def passed(which, back, needed):
        @pl.when((cell >= back) & needed)
        def _():
            for slot in range(SIDE):
                block = held(which, back, slot)
                pltpu.make_async_copy(block, block, pass_recv.at[which, back - 1, slot]).wait()

    beside = mine + 1 - 2 * lax.rem(mine, 2)
    across = mine + 2 - 4 * (mine // 2)
    diagonal = SIDE - 1 - mine

    def share(group, to):
        block = qcat.at[group, :, pl.ds(0, width)]
        return pltpu.make_async_remote_copy(
            src_ref=block,
            dst_ref=block,
            send_sem=share_send.at[to],
            recv_sem=share_recv.at[group],
            device_id={"blk": quarter + to},
            device_id_type=MESH,
        )

    def shared(group):
        block = qcat.at[group, :, pl.ds(0, width)]
        pltpu.make_async_copy(block, block, share_recv.at[group]).wait()

    def share_own():
        for slot in range(SIDE):
            dealt(QUERIES, slot)
        share(mine, across).start()
        share(mine, beside).start()

    first_passes(KEYS)
    share_own()
    first_passes(VALUES)
    shared(across)
    hand_on = pltpu.make_async_remote_copy(
        src_ref=qcat.at[across, :, pl.ds(0, width)],
        dst_ref=qcat.at[across, :, pl.ds(0, width)],
        send_sem=share_send.at[diagonal],
        recv_sem=share_recv.at[across],
        device_id={"blk": quarter + beside},
        device_id_type=MESH,
    )
    hand_on.start()
    passed(KEYS, 1, True)
    passed(KEYS, 2, mine > 0)

    to_log2 = LOG2E / math.sqrt(width)

    def fold(combine, tile):
        return functools.reduce(combine, [tile[at : at + 8] for at in range(0, rows, 8)])

    def attend(first, pairs, await_values):
        group = mine if pairs == 3 else lax.rem(first + mine, SIDE)
        best = [jnp.full((8, rows), 2 * NEG, jnp.float32)] * SIDE
        for pair in range(pairs):
            m = first + pair * SIDE
            scores = lax.dot_general(
                kcat[(m + mine) // SIDE],
                qcat[group],
                (((1,), (1,)), ((), ())),
                preferred_element_type=jnp.float32,
            )
            for part in range(SIDE):
                for piece in range(SIDE):
                    shifted = (
                        scores[piece * rows : (piece + 1) * rows, part * rows : (part + 1) * rows]
                        * to_log2
                        + table[m * SIDE + part - piece + SIDE - 1]
                    )
                    shifts[pair, pl.ds(piece * rows, rows), pl.ds(part * rows, rows)] = shifted
                    best[part] = jnp.maximum(best[part], fold(jnp.maximum, shifted))
        tops = [jnp.max(tile, axis=0, keepdims=True) for tile in best]
        totals = [jnp.zeros((8, rows), jnp.float32)] * SIDE
        weighed = []
        for pair in range(pairs):
            probs = []
            for part in range(SIDE):
                weights = []
                for piece in range(SIDE):
                    shifted = shifts[pair, pl.ds(piece * rows, rows), pl.ds(part * rows, rows)]
                    weight = jnp.exp2(shifted - tops[part])
                    totals[part] = totals[part] + fold(jnp.add, weight)
                    weights.append(weight.astype(jnp.bfloat16))
                probs.append(jnp.concatenate(weights, axis=0))
            weighed.append(jnp.concatenate(probs, axis=1))
        await_values()
        for pair in range(pairs):
            m = first + pair * SIDE
            product = jnp.dot(
                vbuf[(m + mine) // SIDE],
                weighed[pair],
                preferred_element_type=jnp.float32,
            )
            acc[...] = product if pair == 0 else acc[...] + product
        for part in range(SIDE):
            total = jnp.sum(totals[part], axis=0, keepdims=True)
            level = tops[part] + jnp.log2(total)
            at = pl.ds(part * rows, rows)
            if pairs == 3:
                kept[:, at] = acc[:, at] / total
            else:
                part_out[group, :, at] = (acc[:, at] / total).astype(jnp.bfloat16)
            stat_out[group, pl.ds(part, 1), :] = level

    def hand_over(group):
        parts = [
            pltpu.make_async_remote_copy(
                src_ref=part_out.at[group, :, pl.ds(part * rows, rows)],
                dst_ref=part_in.at[mine, :, pl.ds(part * rows, rows)],
                send_sem=part_send.at[group, part],
                recv_sem=part_recv.at[mine, part],
                device_id={"blk": quarter + group},
                device_id_type=MESH,
            )
            for part in range(SIDE)
        ]
        stat = pltpu.make_async_remote_copy(
            src_ref=stat_out.at[group],
            dst_ref=stat_in.at[mine],
            send_sem=stat_send.at[group],
            recv_sem=stat_recv.at[mine],
            device_id={"blk": quarter + group},
            device_id_type=MESH,
        )
        return [stat] + parts

    def turn(order, _):
        group = order + (order >= mine).astype(jnp.int32)

        @pl.when(group != across)
        def _():
            shared(group)

        def await_values():
            passed(VALUES, 1, order == 0)
            passed(VALUES, 2, (order == 0) & (mine > 0))

        attend(lax.rem(group - mine + SIDE, SIDE), 2, await_values)
        for copy in hand_over(group):
            copy.start()
        return 0

    lax.fori_loop(0, SIDE - 1, turn, 0)

    passed(KEYS, 2, mine == 0)
    attend(0, 3, lambda: passed(VALUES, 2, mine == 0))

    others = [lax.rem(mine + step, SIDE) for step in range(1, SIDE)]
    for other in others:
        block = stat_in.at[other]
        pltpu.make_async_copy(block, block, stat_recv.at[other]).wait()

    def home(part):
        src = merged.at[pl.ds(part * rows, rows)]
        dst = out_ref.at[:, pl.ds(pl.multiple_of(head * width, width), width)]
        return src, dst, base + mine * SIDE + part

    def send_home(part):
        src, dst, target = home(part)
        return pltpu.make_async_remote_copy(
            src_ref=src,
            dst_ref=dst,
            send_sem=back_send.at[part],
            recv_sem=back_recv.at[head],
            device_id={"blk": target},
            device_id_type=MESH,
        )

    for part in range(SIDE):
        at = pl.ds(part * rows, rows)
        for other in others:
            block = part_in.at[other, :, at]
            pltpu.make_async_copy(block, block, part_recv.at[other, part]).wait()
        values = [kept[:, at]] + [part_in[other, :, at] for other in others]
        levels = [stat_out[mine, pl.ds(part, 1), :]]
        levels += [stat_in[other, pl.ds(part, 1), :] for other in others]
        most = functools.reduce(jnp.maximum, levels)
        shares = [jnp.exp2(level - most) for level in levels]
        total = functools.reduce(jnp.add, shares)
        whole = [v.astype(jnp.float32) * s for v, s in zip(values, shares)]
        whole = functools.reduce(jnp.add, whole) / total
        merged[at, :] = whole.T.astype(jnp.bfloat16)
        src, dst, target = home(part)

        @pl.when(target != me)
        def _():
            send_home(part).start()

        @pl.when(target == me)
        def _():
            pltpu.make_async_copy(src, dst, back_recv.at[head]).start()

    for h in range(SIDE):
        block = out_ref.at[:, pl.ds(h * width, width)]
        pltpu.make_async_copy(block, block, back_recv.at[h]).wait()

    for which in range(3):
        for h in range(SIDE):
            end_deal(which, h)
    share(mine, across).wait_send()
    share(mine, beside).wait_send()
    hand_on.wait_send()
    for which in (KEYS, VALUES):
        for back in (1, 2):

            @pl.when(me + back * CELL < count)
            def _():
                for slot in range(SIDE):
                    pass_on(which, back, slot).wait_send()

    for other in others:
        for copy in hand_over(other):
            copy.wait_send()
    for part in range(SIDE):

        @pl.when(base + mine * SIDE + part != me)
        def _():
            send_home(part).wait_send()


def on_device(query_rows, key_rows, value_rows, kerple_power, kerple_scale, doc_lengths):
    count = lax.axis_size("blk")
    rows, columns = query_rows.shape
    width = columns // SIDE
    span = SIDE * rows
    return pl.pallas_call(
        functools.partial(kernel, rows, width, count),
        out_shape=pltpu.VMEM((rows, columns), jnp.bfloat16),
        in_specs=[pl.BlockSpec(memory_space=pltpu.SMEM)] * 3 + [pl.BlockSpec(memory_space=pl.ANY)] * 3,
        out_specs=pl.BlockSpec(memory_space=pltpu.VMEM),
        scratch_shapes=[
            pltpu.VMEM((rows, columns), jnp.bfloat16),
            pltpu.VMEM((rows, columns), jnp.bfloat16),
            pltpu.VMEM((rows, columns), jnp.bfloat16),
            pltpu.VMEM((SIDE, width, rows), jnp.bfloat16),
            pltpu.VMEM((SIDE, span, 2 * width), jnp.bfloat16),
            pltpu.VMEM((3, span, 2 * width), jnp.bfloat16),
            pltpu.VMEM((3, width, span), jnp.bfloat16),
            pltpu.VMEM((3, span, span), jnp.float32),
            pltpu.VMEM((width, span), jnp.float32),
            pltpu.VMEM((2 * CELL + 2 * SIDE - 1, rows, rows), jnp.float32),
            pltpu.VMEM((SIDE, width, span), jnp.bfloat16),
            pltpu.VMEM((SIDE, 2 * SIDE, rows), jnp.float32),
            pltpu.VMEM((SIDE, width, span), jnp.bfloat16),
            pltpu.VMEM((SIDE, 2 * SIDE, rows), jnp.float32),
            pltpu.VMEM((width, span), jnp.float32),
            pltpu.VMEM((span, width), jnp.bfloat16),
            pltpu.SemaphoreType.DMA((3,)),
            pltpu.SemaphoreType.DMA((3, SIDE)),
            pltpu.SemaphoreType.DMA((3, SIDE)),
            pltpu.SemaphoreType.DMA((2, 2, SIDE)),
            pltpu.SemaphoreType.DMA((2, 2, SIDE)),
            pltpu.SemaphoreType.DMA((SIDE,)),
            pltpu.SemaphoreType.DMA((SIDE,)),
            pltpu.SemaphoreType.DMA((SIDE, SIDE)),
            pltpu.SemaphoreType.DMA((SIDE, SIDE)),
            pltpu.SemaphoreType.DMA((SIDE,)),
            pltpu.SemaphoreType.DMA((SIDE,)),
            pltpu.SemaphoreType.DMA((SIDE,)),
            pltpu.SemaphoreType.DMA((SIDE,)),
        ],
        compiler_params=pltpu.CompilerParams(
            collective_id=0, has_side_effects=True, vmem_limit_bytes=60 * 2**20
        ),
    )(kerple_power, kerple_scale, doc_lengths, query_rows, key_rows, value_rows)


def solution(mesh):
    block = P(("seq", "blk"), "head")
    return jax.shard_map(
        on_device,
        mesh=mesh,
        in_specs=(block, block, block, P("head"), P("head"), P("seq")),
        out_specs=block,
        check_vma=False,
    )
```
